256 devices in a mesh: dp: 8 (over y, core), seq: 32 (over z, x).
Axes of the slice: x: 4, y: 4, z: 8, core: 2. Of those that a mesh axis runs over, the one named last changes fastest.
Arguments:
- glu_out: bfloat16 [8, 4096, 1536], P('dp', 'seq'), may hold values from -8 to 8
- conv_weight: float32 [32, 1536], replicated, may hold values from -1 to 1
- bn_gain: float32 [16, 1536], replicated, may hold values from 0.25 to 1.75
- bn_bias: float32 [16, 1536], replicated, may hold values from -3 to 3
- w_out: bfloat16 [1536, 1536], P(('dp', 'seq')), may hold values from -0.15625 to 0.15625
- cotangent: bfloat16 [8, 4096, 1536], P('dp', 'seq'), may hold values from -8 to 8
- language: int32 [8], P('dp'), may hold values from 0 to 15
- length: int32 [8], P('dp'), may hold values from 256 to 4096, as said below
Outputs:
- block_out: bfloat16 [8, 4096, 1536], P('dp', 'seq')
- weight_grad: float32 [1536, 1536], P(('dp', 'seq'))
- input_grad: bfloat16 [8, 4096, 1536], P('dp', 'seq')
The draws below stay inside these ranges and needn't reach their ends.
Inputs may be any that keep to these rules, and one draw needn't show every extreme that they name: Each length is a multiple of 256; at least one utterance is valid over all 4096 frames.
All inputs are finite; a program needn't handle non-finite values.
Results may differ from the reference program's by a relative error of at most 0.0095.
Values may be sent and summed in bfloat16 or wider, within the bound.
No kernel may reach another device: no remote copies, remote signals or barrier semaphores. Data moves between devices by JAX's collectives and lax.ppermute only.
A program may use at most 64 MiB of HBM per device.

```python
import jax
import jax.numpy as jnp
from jax import lax

D = 1536
KERNEL = 32
LANGS = 16
STEP = 256
UTT_DEV = 1
FRM_DEV = 128
UTTS = 8
FRAMES = 4096


def draw_length(key, part):
    blocks = FRAMES // STEP
    picked = jax.random.randint(jax.random.fold_in(key, 11), (UTTS,), 1, blocks + 1)
    longest = jax.random.randint(jax.random.fold_in(key, 12), (), 0, UTTS)
    picked = jnp.where(jnp.arange(UTTS, dtype=jnp.int32) == longest, blocks, picked)
    return (picked * STEP).astype(jnp.int32)


def steady_part(key, offset_scale, drift_scale):
    offset = jax.random.normal(jax.random.fold_in(key, 21), (UTTS, 1, D), jnp.float32)
    drift = jax.random.normal(jax.random.fold_in(key, 22), (UTTS, 1, D), jnp.float32)
    ramp = (jnp.arange(FRAMES, dtype=jnp.float32) * (2.0 / FRAMES) - 1.0)[None, :, None]
    return offset_scale * offset + drift_scale * drift * ramp


def rough_part(key):
    noise = jax.random.normal(jax.random.fold_in(key, 31), (UTTS, FRAMES, D), jnp.float32)
    return jnp.clip(noise, -6.0, 6.0)


def draw_glu_out(key, part):
    common = steady_part(jax.random.fold_in(key, 41), 0.5, 0.5)
    total = rough_part(jax.random.fold_in(key, 42)) + common
    return jnp.clip(total, -8.0, 8.0).astype(jnp.bfloat16)


def draw_cotangent(key, part):
    common = steady_part(jax.random.fold_in(key, 51), 0.5, 0.5)
    rough = rough_part(jax.random.fold_in(key, 52))
    groups = UTTS * FRAMES // (UTT_DEV * FRM_DEV)
    width = D // groups
    order = jax.random.permutation(jax.random.fold_in(key, 53), groups)
    utt_index = jnp.arange(UTTS, dtype=jnp.int32)[:, None, None]
    frame_index = jnp.arange(FRAMES, dtype=jnp.int32)[None, :, None]
    group = utt_index // UTT_DEV * (FRAMES // FRM_DEV) + frame_index // FRM_DEV
    column_block = (jnp.arange(D, dtype=jnp.int32) // width)[None, None, :]
    factor = jnp.where(order[group] == column_block, 4.0, 1.0)
    total = rough * factor + common
    return jnp.clip(total, -8.0, 8.0).astype(jnp.bfloat16)


def set_ends(entries, own_key, smallest, high):
    dims = entries.shape
    index_at = [jax.random.randint(jax.random.fold_in(own_key, axis), (), 0, dims[axis]) for axis in range(len(dims))]
    entries = entries.at[tuple(index_at)].set(smallest)
    longest = dims.index(max(dims))
    index_at[longest] = (index_at[longest] + 1) % dims[longest]
    return entries.at[tuple(index_at)].set(high)


def block_scale(own_key, shape, shards, smallest, largest):
    gain = 1.0
    for dim, blocks in shards:
        draws = jax.random.uniform(jax.random.fold_in(jax.random.fold_in(own_key, 6), dim), (blocks,), jnp.float32, smallest / len(shards), largest / len(shards))
        gain = gain * jnp.repeat(jnp.exp(draws), shape[dim] // blocks).reshape((-1,) + (1,) * (len(shape) - 1 - dim))
    return gain


def gaussian(key, extent, scale, most, split=(), kind=jnp.bfloat16):
    gain = block_scale(key, extent, split, -0.22, 0.18) if split else 1.0
    result = jax.random.normal(key, extent, jnp.float32) * scale * gain
    return jnp.minimum(jnp.maximum(result, -most), most).astype(kind)


def setup_inputs(seed: int = 0) -> dict:
    key_of = jax.random.split(jax.random.key(seed), 9)
    return {
        "glu_out": draw_glu_out(jax.random.fold_in(key_of[8], 71), 0),
        "conv_weight": gaussian(key_of[1], (KERNEL, D), KERNEL ** -0.5, 1.0, (), jnp.float32),
        "bn_gain": jnp.clip(1.0 + 0.15 * jax.random.normal(key_of[2], (LANGS, D), jnp.float32), 0.25, 1.75),
        "bn_bias": gaussian(key_of[3], (LANGS, D), 0.5, 3.0, (), jnp.float32),
        "w_out": gaussian(key_of[4], (D, D), D ** -0.5, 0.15625, ((0, 256),)),
        "cotangent": draw_cotangent(jax.random.fold_in(key_of[8], 71), 0),
        "language": set_ends(jax.random.randint(key_of[6], (UTTS,), 0, LANGS), jax.random.fold_in(key_of[6], 1), 0, LANGS - 1).astype(jnp.int32),
        "length": draw_length(jax.random.fold_in(key_of[8], 71), 0),
    }


epsilon = 1e-05

def depthwise(padded, taps, frames):
    running = jnp.zeros((frames, padded.shape[1]), jnp.float32)
    for offset in range(taps.shape[0]):
        running = running + padded[offset:offset + frames].astype(jnp.float32) * taps[offset]
    return running

def prepare(glu_row, length_row, conv_weight):
    valid = (jnp.arange(FRAMES, dtype=jnp.int32) < length_row).astype(jnp.float32)[:, None]
    masked = glu_row * valid.astype(jnp.bfloat16)
    half_width = KERNEL // 2
    padded = jnp.pad(masked, ((half_width, half_width - 1), (0, 0)))
    return (depthwise(padded, conv_weight, FRAMES), valid)

def reference(glu_out, conv_weight, bn_gain, bn_bias, w_out, cotangent, language, length):
    half_width = KERNEL // 2
    one_hot = (language[:, None] == jnp.arange(LANGS, dtype=jnp.int32)[None, :]).astype(jnp.float32)

    def first_pass(inputs):
        convolved, valid = prepare(inputs[0], inputs[1], conv_weight)
        return lax.optimization_barrier(jnp.sum(convolved * valid, axis=0))
    sums = lax.map(first_pass, (glu_out, length))
    counts = jnp.dot(one_hot.T, length.astype(jnp.float32), precision=lax.Precision.HIGHEST)
    denominator = jnp.maximum(counts, 1.0)[:, None]
    average = jnp.dot(one_hot.T, sums, precision=lax.Precision.HIGHEST) / denominator
    average_rows = average[language]

    def second_pass(inputs):
        convolved, valid = prepare(inputs[0], inputs[1], conv_weight)
        centred = (convolved - inputs[2]) * valid
        return lax.optimization_barrier(jnp.sum(centred * centred, axis=0))
    spread = lax.map(second_pass, (glu_out, length, average_rows))
    variance = jnp.dot(one_hot.T, spread, precision=lax.Precision.HIGHEST) / denominator
    inverse_std = lax.rsqrt(variance + epsilon)
    inverse_rows = inverse_std[language]
    gain_rows = bn_gain[language]
    bias_rows = bn_bias[language]

    def third_pass(carry, inputs):
        glu_row, length_row, grad_row, average_row, inverse_row, gain_row, bias_row = inputs
        convolved, valid = prepare(glu_row, length_row, conv_weight)
        normed = (convolved - average_row) * inverse_row
        pre_act = normed * gain_row + bias_row
        sigmoid_act = jax.nn.sigmoid(pre_act)
        active = (pre_act * sigmoid_act * valid).astype(jnp.bfloat16)
        output = jnp.dot(active, w_out, preferred_element_type=jnp.float32).astype(jnp.bfloat16)
        back_proj = lax.dot_general(grad_row, w_out, (((1,), (1,)), ((), ())), preferred_element_type=jnp.float32)
        grad_pre = back_proj * valid * sigmoid_act * (1.0 + pre_act * (1.0 - sigmoid_act))
        grad_normed = grad_pre * gain_row
        carry = carry + lax.dot_general(active, grad_row, (((0,), (0,)), ((), ())), preferred_element_type=jnp.float32)
        return (carry, (output, grad_normed, lax.optimization_barrier(jnp.sum(grad_normed, axis=0)), lax.optimization_barrier(jnp.sum(grad_normed * normed, axis=0))))
    weight_grad, (block_out, grad_all, first_rows, second_rows) = lax.scan(third_pass, jnp.zeros((D, D), jnp.float32), (glu_out, length, cotangent, average_rows, inverse_rows, gain_rows, bias_rows))
    first_sum = jnp.dot(one_hot.T, first_rows, precision=lax.Precision.HIGHEST) / denominator
    second_sum = jnp.dot(one_hot.T, second_rows, precision=lax.Precision.HIGHEST) / denominator

    def fourth_pass(inputs):
        glu_row, length_row, grad_normed, average_row, inverse_row, first_row, second_row = inputs
        convolved, valid = prepare(glu_row, length_row, conv_weight)
        normed = (convolved - average_row) * inverse_row
        grad_conv = (valid * inverse_row * (grad_normed - first_row - normed * second_row)).astype(jnp.bfloat16)
        padded = jnp.pad(grad_conv, ((half_width - 1, half_width), (0, 0)))
        return (depthwise(padded, conv_weight[::-1], FRAMES) * valid).astype(jnp.bfloat16)
    input_grad = lax.map(fourth_pass, (glu_out, length, grad_all, average_rows, inverse_rows, first_sum[language], second_sum[language]))
    return (block_out, weight_grad, input_grad)
```

```python
import jax
import jax.numpy as jnp
from jax import lax
from jax.sharding import Mesh, PartitionSpec as P

LANGS = 16
EPSILON = 1e-05
F32 = jnp.float32
BF16 = jnp.bfloat16
AXES = {"y": 4, "c": 2, "z": 8, "x": 4}
STATS = ("c", "z", "y")


def gather_all(block, axes):
    size = 1
    for axis in axes:
        size *= AXES[axis]
    copies = jnp.broadcast_to(block[None], (size,) + block.shape)
    return lax.all_to_all(copies, axes, 0, 0, tiled=True)


def swap_xy(block):
    pairs = [(y * 4 + x, x * 4 + y) for y in range(4) for x in range(4)]
    return lax.ppermute(block, ("y", "x"), pairs)


def along_z(block, width):
    up = [(i, i + 1) for i in range(AXES["z"] - 1)]
    down = [(i + 1, i) for i in range(AXES["z"] - 1)]
    before = lax.ppermute(block[-width:], "z", up)
    after = lax.ppermute(block[:width], "z", down)
    return before, after


def depthwise(padded, taps, frames, start):
    running = jnp.zeros((frames, padded.shape[1]), F32)
    for offset in range(taps.shape[0]):
        running = running + padded[start + offset : start + offset + frames].astype(F32) * taps[offset]
    return running


def pack(rows):
    lanes = 128
    packed = jnp.concatenate([row.reshape(-1, lanes) for row in rows], axis=0)
    return jnp.pad(packed, ((0, 8 - packed.shape[0]), (0, 0)))


def on_device(glu_out, conv_weight, bn_gain, bn_bias, w_out, cotangent, language, length):
    glu, cot = glu_out[0], cotangent[0]
    own_frames, channels = glu.shape
    kernel = conv_weight.shape[0]
    half = kernel // 2
    parts = AXES["x"]
    block = channels // parts
    frames = own_frames * parts
    column = lax.axis_index("x") * block
    z = lax.axis_index("z")
    own_language, own_length = language[0], length[0]
    taps = lax.dynamic_slice_in_dim(conv_weight, column, block, 1)
    gain = lax.dynamic_slice(bn_gain, (own_language, column), (1, block))
    bias = lax.dynamic_slice(bn_bias, (own_language, column), (1, block))

    wide = frames + 2 * half
    position = z * frames - half + lax.iota(jnp.int32, wide)
    valid = ((position >= 0) & (position < own_length)).astype(F32)[:, None]
    valid_own = valid[half : half + frames]

    mine = lax.all_to_all(glu.reshape(own_frames, parts, block).transpose(1, 0, 2), "x", 0, 0, tiled=True)
    mine = mine.reshape(frames, block) * valid_own.astype(BF16)
    before, after = along_z(mine, 2 * half)
    padded = jnp.concatenate([before, mine, after], axis=0)
    convolved = depthwise(padded, taps, wide, 0)

    cot_rows = gather_all(cot, ("x",)).reshape(frames, channels)
    weight = gather_all(swap_xy(w_out), ("z", "y")).reshape(-1, channels)
    weight = gather_all(weight, ("c",)).reshape(block, channels)
    back_own = lax.dot_general(cot_rows, weight, (((1,), (1,)), ((), ())), preferred_element_type=F32)
    back_before, back_after = along_z(back_own, half)
    back_proj = jnp.concatenate([back_before, back_own, back_after], axis=0)

    own = convolved[half : half + frames]
    own_count = jnp.clip(own_length - z * frames, 0, frames).astype(F32)
    own_sum = jnp.sum(own * valid_own, axis=0)
    own_mean = own_sum / jnp.maximum(own_count, 1.0)
    own_spread = jnp.sum(jnp.square((own - own_mean) * valid_own), axis=0)
    facts = jnp.where(
        lax.iota(jnp.int32, 128) == 0, own_language.astype(F32), own_count
    )
    gathered = gather_all(pack([own_mean, own_spread, facts]), STATS)
    gathered = gathered.reshape(-1, 8, 128)
    rows = block // 128
    means = gathered[:, :rows].reshape(-1, block)
    spreads = gathered[:, rows : 2 * rows].reshape(-1, block)
    same = (gathered[:, 2 * rows, :1] == own_language.astype(F32)).astype(F32)
    counts = gathered[:, 2 * rows, 1:2] * same
    denominator = jnp.maximum(jnp.sum(counts), 1.0)
    average = jnp.sum(means * counts, axis=0) / denominator
    variance = jnp.sum(spreads * same + counts * jnp.square(means - average), axis=0) / denominator
    inverse = lax.rsqrt(variance + EPSILON)

    normed = (convolved - average) * inverse
    pre_act = normed * gain + bias
    gate = jax.nn.sigmoid(pre_act)
    active = (pre_act * gate * valid)[half : half + frames].astype(BF16)
    grad_normed = back_proj * valid * gate * (1.0 + pre_act * (1.0 - gate)) * gain
    grad_own = grad_normed[half : half + frames]
    first = jnp.sum(grad_own, axis=0)
    second = jnp.sum(grad_own * normed[half : half + frames], axis=0)
    sums = gather_all(pack([first, second]), STATS).reshape(-1, 8, 128)
    sums = jnp.sum(sums * same[:, :, None], axis=0) / denominator
    first_sum = sums[:rows].reshape(block)
    second_sum = sums[rows : 2 * rows].reshape(block)
    grad_conv = (valid * inverse * (grad_normed - first_sum - normed * second_sum)).astype(BF16)
    input_grad = (depthwise(grad_conv, taps[::-1], frames, 1) * valid_own).astype(BF16)
    input_grad = lax.all_to_all(input_grad.reshape(parts, own_frames, block), "x", 0, 0, tiled=True)
    input_grad = input_grad.reshape(parts, own_frames, block).transpose(1, 0, 2).reshape(own_frames, channels)

    partial = jnp.dot(active, weight, preferred_element_type=F32).astype(BF16)
    partial = lax.all_to_all(partial.reshape(parts, own_frames, channels), "x", 0, 0, tiled=True)
    output = jnp.sum(partial.reshape(parts, own_frames, channels).astype(F32), axis=0).astype(BF16)

    product = lax.dot_general(active, cot_rows, (((0,), (0,)), ((), ())), preferred_element_type=F32)
    product = product.astype(BF16).reshape(2, block // 2, channels)
    product = lax.all_to_all(product, "c", 0, 0, tiled=True).astype(F32)
    product = jnp.sum(product, axis=0).astype(BF16).reshape(32, -1, channels)
    product = lax.all_to_all(product, ("z", "y"), 0, 0, tiled=True).astype(F32)
    weight_grad = swap_xy(jnp.sum(product, axis=0))
    return output[None], weight_grad, input_grad[None]


def solution(mesh):
    fine = Mesh(mesh.devices.reshape(tuple(AXES.values())), tuple(AXES))
    dp, seq = ("y", "c"), ("z", "x")
    placed = (
        P(dp, seq, None),
        P(),
        P(),
        P(),
        P(dp + seq, None),
        P(dp, seq, None),
        P(dp),
        P(dp),
    )
    return jax.shard_map(
        on_device,
        mesh=fine,
        in_specs=placed,
        out_specs=(P(dp, seq, None), P(dp + seq, None), P(dp, seq, None)),
        check_vma=False,
    )
```

```python
import jax
import jax.numpy as jnp
from jax import lax
from jax.experimental import pallas as pl
from jax.experimental.pallas import tpu as pltpu
from jax.sharding import Mesh, PartitionSpec as P

EPSILON = 1e-05
F32 = jnp.float32
BF16 = jnp.bfloat16
AXES = {"y": 4, "c": 2, "z": 8, "x": 4}
STATS = ("c", "z", "y")
MEMBERS = 64
LANES = 128
PARTS = 4
OWN = 128
FRAMES = 512
BLOCK = 384
TILES = BLOCK // LANES
CHANNELS = 1536
TAPS = 32
HALF = 16
WIDE = FRAMES + 2 * HALF
ROWS = 6
SLOT = 8
SHARE = 192
LIMIT = 12 * 1024 * 1024


def call(body, outs, scratch=(), scalars=1):
    def run(*operands):
        specs = [pl.BlockSpec(memory_space=pltpu.SMEM)] * scalars
        specs += [pl.BlockSpec(memory_space=pltpu.VMEM)] * (len(operands) - scalars)
        return pl.pallas_call(
            body,
            out_shape=[jax.ShapeDtypeStruct(shape, kind) for shape, kind in outs],
            in_specs=specs,
            out_specs=[pl.BlockSpec(memory_space=pltpu.VMEM)] * len(outs),
            scratch_shapes=list(scratch),
            compiler_params=pltpu.CompilerParams(vmem_limit_bytes=LIMIT),
            cost_estimate=pl.CostEstimate(flops=1000, bytes_accessed=1000, transcendentals=0),
        )(*operands)

    return run


def dot(a, b, dims):
    return lax.dot_general(a, b, (dims, ((), ())), preferred_element_type=F32)


def at(index, size):
    return pl.ds(pl.multiple_of(index * size, size), size)


def valid_rows(start, count, length):
    position = start + lax.broadcasted_iota(jnp.int32, (count, LANES), 0)
    return (position >= 0) & (position < length)


def filter_rows(source, lane, taps, row, count, offsets):
    total = jnp.zeros((count, LANES), F32)
    for phase in range(8):
        chosen = [o for o in offsets if o % 8 == phase]
        reach = max(chosen) - phase
        window = source[row + phase : row + phase + count + reach, lane]
        for o in chosen:
            total = total + window[o - phase : o - phase + count] * taps[offsets[o]][None, :]
    return total


def conv_body(facts, first, second, third, fourth, before, after, weights, convolved, payload, padded):
    x, z, length, language = facts[0], facts[1], facts[2], facts[3]
    begin = z * FRAMES - TAPS
    for t in range(TILES):
        lane = slice(t * LANES, (t + 1) * LANES)
        for k, piece in enumerate((first, second, third, fourth)):
            j = lax.rem(x - k + PARTS, PARTS)
            keep = valid_rows(z * FRAMES + j * OWN, OWN, length)
            rows = pl.ds(pl.multiple_of(TAPS + j * OWN, TAPS), OWN)
            padded[rows, lane] = jnp.where(keep, piece[:, lane].astype(F32), 0.0)
        padded[0:TAPS, lane] = jnp.where(valid_rows(begin, TAPS, length), before[:, lane].astype(F32), 0.0)
        padded[TAPS + FRAMES :, lane] = jnp.where(
            valid_rows(begin + TAPS + FRAMES, TAPS, length), after[:, lane].astype(F32), 0.0
        )
    step = WIDE // 4
    for t in range(TILES):
        lane = slice(t * LANES, (t + 1) * LANES)
        taps = weights[:, pl.ds(pl.multiple_of(x * BLOCK + t * LANES, LANES), LANES)]

        for row in range(0, WIDE, step):
            convolved[row : row + step, lane] = filter_rows(
                padded, lane, taps, row, step, {k: k for k in range(TAPS)}
            )

    count = jnp.clip(length - z * FRAMES, 0, FRAMES).astype(F32)
    keep = valid_rows(z * FRAMES, FRAMES, length)
    lines = []
    spreads = []
    for t in range(TILES):
        lane = slice(t * LANES, (t + 1) * LANES)
        values = convolved[HALF : HALF + FRAMES, lane]
        mean = jnp.sum(jnp.where(keep, values, 0.0), axis=0, keepdims=True) / jnp.maximum(count, 1.0)
        centred = jnp.where(keep, values - mean, 0.0)
        lines.append(mean)
        spreads.append(jnp.sum(centred * centred, axis=0, keepdims=True))
    ones = jnp.ones((1, LANES), F32)
    message = jnp.concatenate(lines + spreads + [ones * language.astype(F32), ones * count], axis=0)
    payload[...] = jnp.broadcast_to(message[None], (MEMBERS, 8, LANES))


def back_body(facts, first, second, third, fourth, own_half, other_half, weight, back, low, high):
    x, core = facts[0], facts[4]
    weight[at(core, SHARE), :] = own_half[...]
    weight[at(1 - core, SHARE), :] = other_half[...]
    for k, piece in enumerate((first, second, third, fourth)):
        j = lax.rem(x - k + PARTS, PARTS)
        back[at(j, OWN), :] = dot(piece[...], weight[...], ((1,), (1,)))
    low[...] = back[0:HALF, :]
    high[...] = back[FRAMES - HALF :, :]


def combine(gathered, language):
    same = gathered[:, 6, :] == language.astype(F32)
    counts = jnp.where(same, gathered[:, 7, :], 0.0)
    total = jnp.maximum(jnp.sum(counts, axis=0, keepdims=True), 1.0)
    return same, counts, total


def chosen_row(table, index):
    here = lax.broadcasted_iota(jnp.int32, table.shape, 0) == index
    return jnp.sum(jnp.where(here, table, 0.0), axis=0, keepdims=True)


def act_body(facts, gathered, convolved, back, before, after, gains, biases, active, normed, grad, inverses, payload):
    x, z, length, language = facts[0], facts[1], facts[2], facts[3]
    same, counts, total = combine(gathered, language)
    spans = ((0, HALF), (HALF, FRAMES), (HALF + FRAMES, HALF))
    sums = [None] * 8
    sums[6] = sums[7] = jnp.zeros((1, LANES), F32)
    kept = []
    for t in range(TILES):
        lane = slice(t * LANES, (t + 1) * LANES)
        wide_lane = pl.ds(pl.multiple_of(x * BLOCK + t * LANES, LANES), LANES)
        means = gathered[:, t, :]
        average = jnp.sum(means * counts, axis=0, keepdims=True) / total
        spread = jnp.where(same, gathered[:, TILES + t, :], 0.0)
        away = means - average
        variance = jnp.sum(spread + counts * (away * away), axis=0, keepdims=True) / total
        inverse = lax.rsqrt(variance + EPSILON)
        kept.append(inverse)
        gain = chosen_row(gains[:, wide_lane], language)
        bias = chosen_row(biases[:, wide_lane], language)
        for part, (row, size) in enumerate(spans):
            step = min(size, 128)
            first = second = jnp.zeros((1, LANES), F32)
            for at_row in range(0, size, step):
                here = slice(row + at_row, row + at_row + step)
                keep = valid_rows(z * FRAMES - HALF + row + at_row, step, length)
                value = (convolved[here, lane] - average) * inverse
                pre = value * gain + bias
                gate = 1.0 / (1.0 + jnp.exp(-pre))
                source = (before, back, after)[part]
                upstream = source[at_row : at_row + step, lane]
                slope = jnp.where(keep, upstream * gate * (1.0 + pre * (1.0 - gate)), 0.0) * gain
                normed[here, lane] = value
                grad[here, lane] = slope
                if part == 1:
                    active[at_row : at_row + step, lane] = jnp.where(keep, pre * gate, 0.0).astype(BF16)
                    first = first + jnp.sum(slope, axis=0, keepdims=True)
                    second = second + jnp.sum(slope * value, axis=0, keepdims=True)
            if part == 1:
                sums[t], sums[TILES + t] = first, second
    payload[...] = jnp.broadcast_to(jnp.concatenate(sums, axis=0)[None], (MEMBERS, 8, LANES))
    inverses[...] = jnp.concatenate(kept + [sums[6]] * (8 - TILES), axis=0)


def grad_body(facts, gathered, sums, normed, grad, inverses, weights, first, second, third, fourth, rounded, result):
    x, z, length, language = facts[0], facts[1], facts[2], facts[3]
    same, counts, total = combine(gathered, language)
    keep = valid_rows(z * FRAMES - HALF, WIDE, length)
    step = FRAMES // 4
    for t in range(TILES):
        lane = slice(t * LANES, (t + 1) * LANES)
        shift = jnp.sum(jnp.where(same, sums[:, t, :], 0.0), axis=0, keepdims=True) / total
        scale = jnp.sum(jnp.where(same, sums[:, TILES + t, :], 0.0), axis=0, keepdims=True) / total
        inverse = inverses[t : t + 1, :]
        value = inverse * (grad[:, lane] - shift - normed[:, lane] * scale)
        rounded[:, lane] = jnp.where(keep, value, 0.0).astype(BF16).astype(F32)
    for t in range(TILES):
        lane = slice(t * LANES, (t + 1) * LANES)
        taps = weights[:, pl.ds(pl.multiple_of(x * BLOCK + t * LANES, LANES), LANES)]

        for row in range(0, FRAMES, step):
            value = filter_rows(rounded, lane, taps, row, step, {TAPS - k: k for k in range(TAPS)})
            inside = valid_rows(z * FRAMES + row, step, length)
            result[row : row + step, lane] = jnp.where(inside, value, 0.0)

    for k, piece in enumerate((first, second, third, fourth)):
        j = lax.rem(x + k, PARTS)
        piece[...] = result[at(j, OWN), :].astype(BF16)


def lanes_body(facts, first, second, third, fourth, joined):
    x = facts[0]
    for k, piece in enumerate((first, second, third, fourth)):
        j = lax.rem(x - k + PARTS, PARTS)
        joined[:, pl.ds(pl.multiple_of(j * BLOCK, LANES), BLOCK)] = piece[...]


def out_body(facts, active, weight, kept, first, second, third):
    x = facts[0]
    kept[...] = dot(active[at(x, OWN), :], weight[...], ((1,), (0,)))
    for k, piece in enumerate((first, second, third)):
        j = lax.rem(x + k + 1, PARTS)
        piece[...] = dot(active[at(j, OWN), :], weight[...], ((1,), (0,))).astype(BF16)


def product_body(facts, active, first, second, third, fourth, kept, sent, total):
    x, core = facts[0], facts[4]
    for k, piece in enumerate((first, second, third, fourth)):
        j = lax.rem(x - k + PARTS, PARTS)
        part = dot(active[at(j, OWN), :], piece[...], ((0,), (0,)))
        total[...] = part if k == 0 else total[...] + part
    kept[...] = total[at(core, SHARE), :]
    sent[...] = total[at(1 - core, SHARE), :].astype(BF16)


def slots():
    local = lax.broadcasted_iota(jnp.int32, (SHARE, 1), 0)
    slot = local // ROWS * SLOT + lax.rem(local, ROWS)
    return (lax.broadcasted_iota(jnp.int32, (SHARE, SHARE // ROWS * SLOT), 1) == slot).astype(BF16)


def weight_body(rows, half):
    half[...] = dot(slots(), rows[...], ((1,), (0,))).astype(BF16)


def spread_body(kept, other, spread):
    both = (kept[...] + other[...].astype(F32)).astype(BF16)
    spread[...] = dot(slots(), both, ((0,), (0,))).astype(BF16)


def around_x(piece, shift):
    size = AXES["x"]
    return lax.ppermute(piece, "x", [(i, (i + shift) % size) for i in range(size)])


def other_core(block):
    return lax.ppermute(block, "c", [(0, 1), (1, 0)])


def swap_xy(block):
    pairs = [(y * 4 + x, x * 4 + y) for y in range(4) for x in range(4)]
    return lax.ppermute(block, ("y", "x"), pairs)


def wait_for(value, *others):
    return lax.optimization_barrier((value,) + others)[0]


def along_z(low, high):
    up = [(i, i + 1) for i in range(AXES["z"] - 1)]
    down = [(i + 1, i) for i in range(AXES["z"] - 1)]
    return lax.ppermute(high, "z", up), lax.ppermute(low, "z", down)


def exchange(payload, axes):
    return lax.all_to_all(payload, axes, 0, 0, tiled=True)


def on_device(glu_out, conv_weight, bn_gain, bn_bias, w_out, cotangent, language, length):
    glu, cot = glu_out[0], cotangent[0]
    x, y, z, core = (lax.axis_index(axis) for axis in ("x", "y", "z", "c"))
    facts = jnp.stack([x, z, length[0], language[0], core, y]).astype(jnp.int32)

    pieces = [lax.dynamic_slice(glu, (0, lax.rem(x + k, PARTS) * BLOCK), (OWN, BLOCK)) for k in range(PARTS)]
    pieces = [pieces[0]] + [around_x(pieces[k], k) for k in range(1, PARTS)]
    later = wait_for(cot, *pieces)
    cots = [cot] + [around_x(later, k) for k in range(1, PARTS)]
    low = jnp.stack([piece[:TAPS] for piece in pieces])
    high = jnp.stack([piece[OWN - TAPS :] for piece in pieces])
    low = lax.dynamic_index_in_dim(low, x, 0, keepdims=False)
    high = lax.dynamic_index_in_dim(high, lax.rem(x + 1, PARTS), 0, keepdims=False)
    before, after = along_z(low, high)
    convolved, payload = call(
        conv_body,
        [((WIDE, BLOCK), F32), ((MEMBERS, 8, LANES), F32)],
        [pltpu.VMEM((WIDE + 2 * HALF, BLOCK), F32)],
    )(facts, *pieces, before, after, conv_weight)

    slot = jnp.broadcast_to(swap_xy(w_out)[None], (32, ROWS, CHANNELS))
    slot = jnp.pad(slot, ((0, 0), (0, SLOT - ROWS), (0, 0))).reshape(-1, CHANNELS)
    rows = exchange(slot, ("z", "y"))
    (half,) = call(weight_body, [((SHARE, CHANNELS), BF16)], scalars=0)(wait_for(rows, payload))
    gathered = exchange(wait_for(payload, *cots), STATS)
    weight, back, low, high = call(
        back_body,
        [((BLOCK, CHANNELS), BF16), ((FRAMES, BLOCK), F32), ((HALF, BLOCK), F32), ((HALF, BLOCK), F32)],
    )(facts, *cots, half, other_core(half))
    back_before, back_after = along_z(low, high)

    active, normed, grad, inverses, payload = call(
        act_body,
        [
            ((FRAMES, BLOCK), BF16),
            ((WIDE, BLOCK), F32),
            ((WIDE, BLOCK), F32),
            ((8, LANES), F32),
            ((MEMBERS, 8, LANES), F32),
        ],
    )(facts, gathered, convolved, back, back_before, back_after, bn_gain, bn_bias)
    sums = exchange(payload, STATS)

    kept, sent = call(
        product_body,
        [((SHARE, CHANNELS), F32), ((SHARE, CHANNELS), BF16)],
        [pltpu.VMEM((BLOCK, CHANNELS), F32)],
    )(facts, active, *cots)
    (spread,) = call(spread_body, [((32 * SLOT, CHANNELS), BF16)], scalars=0)(kept, other_core(sent))
    spread = exchange(spread, ("z", "y")).reshape(32, SLOT, CHANNELS)
    weight_grad = swap_xy(jnp.sum(spread.astype(F32), axis=0)[:ROWS])

    output, *others = call(
        out_body, [((OWN, CHANNELS), F32)] + [((OWN, CHANNELS), BF16)] * (PARTS - 1)
    )(facts, active, weight)
    for k, piece in enumerate(others):
        output = output + around_x(piece, k + 1).astype(F32)
    output = output.astype(BF16)

    pieces = call(
        grad_body,
        [((OWN, BLOCK), BF16)] * PARTS,
        [pltpu.VMEM((WIDE, BLOCK), F32), pltpu.VMEM((FRAMES, BLOCK), F32)],
    )(facts, gathered, sums, normed, grad, inverses, conv_weight)
    pieces = [pieces[0]] + [around_x(pieces[k], k) for k in range(1, PARTS)]
    (input_grad,) = call(lanes_body, [((OWN, CHANNELS), BF16)])(facts, *pieces)
    return output[None], weight_grad, input_grad[None]


def solution(mesh):
    fine = Mesh(mesh.devices.reshape(tuple(AXES.values())), tuple(AXES))
    dp, seq = ("y", "c"), ("z", "x")
    placed = (
        P(dp, seq, None),
        P(),
        P(),
        P(),
        P(dp + seq, None),
        P(dp, seq, None),
        P(dp),
        P(dp),
    )
    return jax.shard_map(
        on_device,
        mesh=fine,
        in_specs=placed,
        out_specs=(P(dp, seq, None), P(dp + seq, None), P(dp, seq, None)),
        check_vma=False,
    )
```

```python
import jax
import jax.numpy as jnp
from jax import lax
from jax.experimental import pallas as pl
from jax.experimental.pallas import tpu as pltpu
from jax.sharding import Mesh, PartitionSpec as P

EPSILON = 1e-05
F32 = jnp.float32
BF16 = jnp.bfloat16
AXES = {"y": 4, "c": 2, "z": 8, "x": 4}
STATS = ("c", "z", "y")
MEMBERS = 64
LANES = 128
PARTS = 4
OWN = 128
FRAMES = 512
BLOCK = 384
TILES = BLOCK // LANES
CHANNELS = 1536
TAPS = 32
HALF = 16
WIDE = FRAMES + 2 * HALF
ROWS = 6
FOLD = 4
SLOT = FOLD * ROWS
SENT = 32 * SLOT
SHARE = 192
STRIP = SHARE // 4
LIMIT = 12 * 1024 * 1024


def call(body, outs, scratch=(), scalars=1, cost=1):
    def run(*operands):
        specs = [pl.BlockSpec(memory_space=pltpu.SMEM)] * scalars
        specs += [pl.BlockSpec(memory_space=pltpu.VMEM)] * (len(operands) - scalars)
        return pl.pallas_call(
            body,
            out_shape=[jax.ShapeDtypeStruct(shape, kind) for shape, kind in outs],
            in_specs=specs,
            out_specs=[pl.BlockSpec(memory_space=pltpu.VMEM)] * len(outs),
            scratch_shapes=list(scratch),
            compiler_params=pltpu.CompilerParams(vmem_limit_bytes=LIMIT),
            cost_estimate=pl.CostEstimate(flops=cost * 10**9, bytes_accessed=1000, transcendentals=0),
        )(*operands)

    return run


def small(body, shape, kind):
    return lambda *operands: call(body, [(shape, kind)], scalars=0)(*operands)[0]


def dot(a, b, dims):
    return lax.dot_general(a, b, (dims, ((), ())), preferred_element_type=F32)


def at(index, size):
    return pl.ds(pl.multiple_of(index * size, size), size)


def valid_rows(start, count, length):
    position = start + lax.broadcasted_iota(jnp.int32, (count, LANES), 0)
    return (position >= 0) & (position < length)


def filter_rows(source, lane, taps, row, count, offsets):
    total = jnp.zeros((count, LANES), F32)
    for phase in range(8):
        chosen = [o for o in offsets if o % 8 == phase]
        reach = max(chosen) - phase
        window = source[row + phase : row + phase + count + reach, lane]
        for o in chosen:
            total = total + window[o - phase : o - phase + count] * taps[offsets[o]][None, :]
    return total


def edge_row(j, low, high, spare):
    return jnp.where(j == 0, low, jnp.where(j == PARTS - 1, high, spare))


def conv_body(facts, first, second, third, fourth, weights, convolved, payload, padded):
    x, z, length, language = facts[0], facts[1], facts[2], facts[3]
    begin = z * FRAMES - TAPS
    for k, piece in enumerate((first, second, third, fourth)):
        j = lax.rem(x - k + PARTS, PARTS)
        main = pl.multiple_of(TAPS + j * OWN, TAPS)
        rim = pl.multiple_of(edge_row(j, 0, TAPS + FRAMES, 2 * TAPS + FRAMES), TAPS)
        for t in range(TILES):
            lane = slice(t * LANES, (t + 1) * LANES)
            keep = valid_rows(begin + main, OWN, length)
            padded[pl.ds(main, OWN), lane] = jnp.where(keep, piece[0:OWN, lane].astype(F32), 0.0)
            keep = valid_rows(begin + rim, TAPS, length)
            padded[pl.ds(rim, TAPS), lane] = jnp.where(keep, piece[OWN : OWN + TAPS, lane].astype(F32), 0.0)
    step = WIDE // 4
    for t in range(TILES):
        lane = slice(t * LANES, (t + 1) * LANES)
        taps = weights[:, pl.ds(pl.multiple_of(x * BLOCK + t * LANES, LANES), LANES)]

        for row in range(0, WIDE, step):
            convolved[row : row + step, lane] = filter_rows(
                padded, lane, taps, row, step, {k: k for k in range(TAPS)}
            )

    count = jnp.clip(length - z * FRAMES, 0, FRAMES).astype(F32)
    keep = valid_rows(z * FRAMES, FRAMES, length)
    lines = []
    spreads = []
    for t in range(TILES):
        lane = slice(t * LANES, (t + 1) * LANES)
        values = convolved[HALF : HALF + FRAMES, lane]
        mean = jnp.sum(jnp.where(keep, values, 0.0), axis=0, keepdims=True) / jnp.maximum(count, 1.0)
        centred = jnp.where(keep, values - mean, 0.0)
        lines.append(mean)
        spreads.append(jnp.sum(centred * centred, axis=0, keepdims=True))
    ones = jnp.ones((1, LANES), F32)
    message = jnp.concatenate(lines + spreads + [ones * language.astype(F32), ones * count], axis=0)
    payload[...] = jnp.broadcast_to(message[None], (MEMBERS, 8, LANES))


def back_body(facts, first, second, third, fourth, own_half, other_half, back, weight):
    x, core = facts[0], facts[4]
    weight[at(core, SHARE), :] = own_half[...]
    weight[at(1 - core, SHARE), :] = other_half[...]
    for k, piece in enumerate((first, second, third, fourth)):
        j = lax.rem(x - k + PARTS, PARTS)
        result = dot(piece[...], weight[...], ((1,), (1,)))
        back[pl.ds(pl.multiple_of(HALF + j * OWN, HALF), OWN), :] = result[0:OWN]
        rim = pl.multiple_of(edge_row(j, 0, HALF + FRAMES, WIDE), HALF)
        back[pl.ds(rim, HALF), :] = result[OWN : OWN + HALF]


def combine(gathered, language):
    same = gathered[:, 6, :] == language.astype(F32)
    counts = jnp.where(same, gathered[:, 7, :], 0.0)
    total = jnp.maximum(jnp.sum(counts, axis=0, keepdims=True), 1.0)
    return same, counts, total


def chosen_row(table, index):
    here = lax.broadcasted_iota(jnp.int32, table.shape, 0) == index
    return jnp.sum(jnp.where(here, table, 0.0), axis=0, keepdims=True)


def act_body(facts, gathered, convolved, back, gains, biases, kept, sent, normed, grad, inverses, payload, active):
    x, z, length, language = facts[0], facts[1], facts[2], facts[3]
    same, counts, total = combine(gathered, language)
    spans = ((0, HALF), (HALF, FRAMES), (HALF + FRAMES, HALF))
    sums = [None] * 8
    sums[6] = sums[7] = jnp.zeros((1, LANES), F32)
    scales = []
    for t in range(TILES):
        lane = slice(t * LANES, (t + 1) * LANES)
        wide_lane = pl.ds(pl.multiple_of(x * BLOCK + t * LANES, LANES), LANES)
        means = gathered[:, t, :]
        average = jnp.sum(means * counts, axis=0, keepdims=True) / total
        spread = jnp.where(same, gathered[:, TILES + t, :], 0.0)
        away = means - average
        variance = jnp.sum(spread + counts * (away * away), axis=0, keepdims=True) / total
        inverse = lax.rsqrt(variance + EPSILON)
        scales.append(inverse)
        gain = chosen_row(gains[:, wide_lane], language)
        bias = chosen_row(biases[:, wide_lane], language)
        for part, (row, size) in enumerate(spans):
            step = min(size, 128)
            first = second = jnp.zeros((1, LANES), F32)
            for at_row in range(0, size, step):
                here = slice(row + at_row, row + at_row + step)
                keep = valid_rows(z * FRAMES - HALF + row + at_row, step, length)
                value = (convolved[here, lane] - average) * inverse
                pre = value * gain + bias
                gate = 1.0 / (1.0 + jnp.exp(-pre))
                upstream = back[here, lane]
                slope = jnp.where(keep, upstream * gate * (1.0 + pre * (1.0 - gate)), 0.0) * gain
                normed[here, lane] = value
                grad[here, lane] = slope
                if part == 1:
                    active[at_row : at_row + step, lane] = jnp.where(keep, pre * gate, 0.0).astype(BF16)
                    first = first + jnp.sum(slope, axis=0, keepdims=True)
                    second = second + jnp.sum(slope * value, axis=0, keepdims=True)
            if part == 1:
                sums[t], sums[TILES + t] = first, second
    payload[...] = jnp.broadcast_to(jnp.concatenate(sums, axis=0)[None], (MEMBERS, 8, LANES))
    first_core = facts[4] == 0
    kept[...] = jnp.where(first_core, active[:, :SHARE], active[:, SHARE:])
    sent[...] = jnp.where(first_core, active[:, SHARE:], active[:, :SHARE])
    inverses[...] = jnp.concatenate(scales + [sums[6]] * (8 - TILES), axis=0)


def grad_body(facts, gathered, sums, normed, grad, inverses, weights, first, second, third, fourth, rounded, result):
    x, z, length, language = facts[0], facts[1], facts[2], facts[3]
    same, counts, total = combine(gathered, language)
    keep = valid_rows(z * FRAMES - HALF, WIDE, length)
    step = FRAMES // 4
    for t in range(TILES):
        lane = slice(t * LANES, (t + 1) * LANES)
        shift = jnp.sum(jnp.where(same, sums[:, t, :], 0.0), axis=0, keepdims=True) / total
        scale = jnp.sum(jnp.where(same, sums[:, TILES + t, :], 0.0), axis=0, keepdims=True) / total
        inverse = inverses[t : t + 1, :]
        value = inverse * (grad[:, lane] - shift - normed[:, lane] * scale)
        rounded[:, lane] = jnp.where(keep, value, 0.0).astype(BF16).astype(F32)
    for t in range(TILES):
        lane = slice(t * LANES, (t + 1) * LANES)
        taps = weights[:, pl.ds(pl.multiple_of(x * BLOCK + t * LANES, LANES), LANES)]

        for row in range(0, FRAMES, step):
            value = filter_rows(rounded, lane, taps, row, step, {TAPS - k: k for k in range(TAPS)})
            inside = valid_rows(z * FRAMES + row, step, length)
            result[row : row + step, lane] = jnp.where(inside, value, 0.0)

    for k, piece in enumerate((first, second, third, fourth)):
        j = lax.rem(x + k, PARTS)
        piece[...] = result[at(j, OWN), :].astype(BF16)


def lanes_body(facts, first, second, third, fourth, joined):
    x = facts[0]
    for k, piece in enumerate((first, second, third, fourth)):
        j = lax.rem(x - k + PARTS, PARTS)
        joined[:, pl.ds(pl.multiple_of(j * BLOCK, LANES), BLOCK)] = piece[...]


def out_body(facts, mine, theirs, own_half, other_half, kept, first, second, third):
    x = facts[0]
    for k, piece in enumerate((kept, first, second, third)):
        rows = at(lax.rem(x + k, PARTS), OWN)
        total = dot(mine[rows, :], own_half[...], ((1,), (0,))) + dot(theirs[rows, :], other_half[...], ((1,), (0,)))
        piece[...] = total.astype(piece.dtype)


def product_body(facts, mine, theirs, first, second, third, fourth, kept, *sent):
    x = facts[0]
    for half in (theirs, mine):
        total = jnp.zeros((SHARE, CHANNELS), F32)
        for k, piece in enumerate((first, second, third, fourth)):
            j = lax.rem(x - k + PARTS, PARTS)
            total = total + dot(half[at(j, OWN), :], piece[0:OWN, :], ((0,), (0,)))
        if half is mine:
            kept[...] = total
        else:
            for n, target in enumerate(sent):
                target[...] = total[n * STRIP : (n + 1) * STRIP].astype(BF16)


def slots(q):
    row = lax.broadcasted_iota(jnp.int32, (SENT, 1), 0)
    inner = lax.rem(row, SLOT)
    wanted = jnp.where(inner // ROWS == q, row // SLOT * ROWS + lax.rem(inner, ROWS), -1)
    return (lax.broadcasted_iota(jnp.int32, (SENT, SHARE), 1) == wanted).astype(BF16)


def tile_at(q, g):
    start = (FOLD * g + q) * LANES
    return slice(start, start + LANES)


def folded(block, q):
    return jnp.concatenate([block[:, tile_at(q, g)] for g in range(TILES)], axis=1)


def copies_body(row_block, copies):
    inner = lax.rem(lax.broadcasted_iota(jnp.int32, (SENT, ROWS), 0), SLOT)
    column = lax.broadcasted_iota(jnp.int32, (SENT, ROWS), 1)
    total = jnp.zeros((SENT, BLOCK), F32)
    for q in range(FOLD):
        choose = (inner == q * ROWS + column).astype(BF16)
        total = total + dot(choose, folded(row_block[...], q), ((1,), (0,)))
    copies[...] = total.astype(BF16)


def weight_body(rows, half):
    for q in range(FOLD):
        part = dot(slots(q), rows[...], ((0,), (0,))).astype(BF16)
        for g in range(TILES):
            half[:, tile_at(q, g)] = part[:, g * LANES : (g + 1) * LANES]


def spread_body(kept, first, second, third, fourth, spread):
    other = jnp.concatenate([strip[...].astype(F32) for strip in (first, second, third, fourth)], axis=0)
    both = (kept[...] + other).astype(BF16)
    total = jnp.zeros((SENT, BLOCK), F32)
    for q in range(FOLD):
        total = total + dot(slots(q), folded(both, q), ((1,), (0,)))
    spread[...] = total.astype(BF16)


def unfold_body(sums, rows):
    for q in range(FOLD):
        for g in range(TILES):
            rows[:, tile_at(q, g)] = sums[q * ROWS : (q + 1) * ROWS, g * LANES : (g + 1) * LANES]


def around_x(piece, shift):
    size = AXES["x"]
    return lax.ppermute(piece, "x", [(i, (i + shift) % size) for i in range(size)])


def other_core(block):
    return lax.ppermute(block, "c", [(0, 1), (1, 0)])


def swap_xy(block):
    pairs = [(y * 4 + x, x * 4 + y) for y in range(4) for x in range(4)]
    return lax.ppermute(block, ("y", "x"), pairs)


def wait_for(value, *others):
    return lax.optimization_barrier((value,) + others)[0]


def between_blocks(rows):
    ends = [(4 * z + 3, 4 * z + 4) for z in range(AXES["z"] - 1)]
    return lax.ppermute(rows, ("z", "x"), ends + [(b, a) for a, b in ends])


def exchange(payload, axes):
    return lax.all_to_all(payload, axes, 0, 0, tiled=True)


def on_device(glu_out, conv_weight, bn_gain, bn_bias, w_out, cotangent, language, length):
    glu, cot = glu_out[0], cotangent[0]
    x, y, z, core = (lax.axis_index(axis) for axis in ("x", "y", "z", "c"))
    facts = jnp.stack([x, z, length[0], language[0], core, y]).astype(jnp.int32)

    last = x == PARTS - 1
    rim = jnp.concatenate(
        [
            lax.dynamic_slice_in_dim(glu, jnp.where(last, OWN - TAPS, 0), TAPS, 0),
            lax.dynamic_slice_in_dim(cot, jnp.where(last, OWN - HALF, 0), HALF, 0),
        ],
        axis=0,
    )
    rim = between_blocks(rim)
    copies = small(copies_body, (SENT, BLOCK), BF16)(swap_xy(w_out))

    pieces = []
    for k in range(PARTS):
        column = lax.rem(x + k, PARTS) * BLOCK
        own = lax.dynamic_slice(glu, (0, column), (OWN, BLOCK))
        piece = jnp.concatenate([own, lax.dynamic_slice(rim, (0, column), (TAPS, BLOCK))], axis=0)
        pieces.append(around_x(piece, k) if k else piece)
    rows = exchange(wait_for(copies, *pieces), ("z", "y"))
    cot = wait_for(jnp.concatenate([cot, rim[TAPS:]], axis=0), *pieces)
    cots = [cot] + [around_x(cot, k) for k in range(1, PARTS)]
    convolved, payload = call(
        conv_body,
        [((WIDE, BLOCK), F32), ((MEMBERS, 8, LANES), F32)],
        [pltpu.VMEM((FRAMES + 3 * TAPS, BLOCK), F32)],
        cost=5,
    )(facts, *pieces, conv_weight)

    (half,) = call(weight_body, [((SHARE, CHANNELS), BF16)], scalars=0)(wait_for(rows, payload))
    gathered = exchange(wait_for(payload, half, *cots), STATS)
    other_half = other_core(half)
    (back,) = call(back_body, [((WIDE + HALF, BLOCK), F32)], [pltpu.VMEM((BLOCK, CHANNELS), BF16)], cost=3)(
        facts, *cots, half, other_half
    )

    kept, sent, normed, grad, inverses, payload = call(
        act_body,
        [
            ((FRAMES, SHARE), BF16),
            ((FRAMES, SHARE), BF16),
            ((WIDE, BLOCK), F32),
            ((WIDE, BLOCK), F32),
            ((8, LANES), F32),
            ((MEMBERS, 8, LANES), F32),
        ],
        [pltpu.VMEM((FRAMES, BLOCK), BF16)],
        cost=2,
    )(facts, gathered, convolved, back, bn_gain, bn_bias)
    sums = exchange(payload, STATS)

    output, *others = call(out_body, [((OWN, CHANNELS), F32)] + [((OWN, CHANNELS), BF16)] * (PARTS - 1))(
        facts, kept, sent, half, other_half
    )
    arrived = [around_x(piece, k + 1) for k, piece in enumerate(others)]

    kept, *sent = call(product_body, [((SHARE, CHANNELS), F32)] + [((STRIP, CHANNELS), BF16)] * 4)(
        facts, wait_for(kept, *others), sent, *cots
    )
    (spread,) = call(spread_body, [((SENT, BLOCK), BF16)], scalars=0)(kept, *[other_core(strip) for strip in sent])
    spread = exchange(spread, ("z", "y")).reshape(32, SLOT, BLOCK)
    spread = swap_xy(jnp.sum(spread.astype(F32), axis=0))
    (weight_grad,) = call(unfold_body, [((ROWS, CHANNELS), F32)], scalars=0)(spread)

    pieces = call(
        grad_body,
        [((OWN, BLOCK), BF16)] * PARTS,
        [pltpu.VMEM((WIDE, BLOCK), F32), pltpu.VMEM((FRAMES, BLOCK), F32)],
        cost=5,
    )(facts, gathered, sums, normed, grad, inverses, conv_weight)
    for piece in arrived:
        output = output + wait_for(piece, *pieces).astype(F32)
    output = output.astype(BF16)
    pieces = [pieces[0]] + [around_x(pieces[k], k) for k in range(1, PARTS)]
    (input_grad,) = call(lanes_body, [((OWN, CHANNELS), BF16)])(facts, *pieces)
    return output[None], weight_grad, input_grad[None]


def solution(mesh):
    fine = Mesh(mesh.devices.reshape(tuple(AXES.values())), tuple(AXES))
    dp, seq = ("y", "c"), ("z", "x")
    placed = (
        P(dp, seq, None),
        P(),
        P(),
        P(),
        P(dp + seq, None),
        P(dp, seq, None),
        P(dp),
        P(dp),
    )
    return jax.shard_map(
        on_device,
        mesh=fine,
        in_specs=placed,
        out_specs=(P(dp, seq, None), P(dp + seq, None), P(dp, seq, None)),
        check_vma=False,
    )
```

```python
import jax
import jax.numpy as jnp
from jax import lax
from jax.experimental import pallas as pl
from jax.experimental.pallas import tpu as pltpu
from jax.sharding import Mesh, PartitionSpec as P

EPSILON = 1e-05
F32 = jnp.float32
BF16 = jnp.bfloat16
AXES = {"y": 4, "c": 2, "z": 8, "x": 4}
STATS = ("c", "z", "y")
MEMBERS = 64
LANES = 128
PARTS = 4
OWN = 128
FRAMES = 512
BLOCK = 384
TILES = BLOCK // LANES
CHANNELS = 1536
TAPS = 32
HALF = 16
WIDE = FRAMES + 2 * HALF
ROWS = 6
FOLD = 4
SLOT = FOLD * ROWS
SENT = 32 * SLOT
SHARE = 192
STRIP = SHARE // 4
LIMIT = 12 * 1024 * 1024


def call(body, outs, scratch=(), scalars=1, cost=1):
    def run(*operands):
        specs = [pl.BlockSpec(memory_space=pltpu.SMEM)] * scalars
        specs += [pl.BlockSpec(memory_space=pltpu.VMEM)] * (len(operands) - scalars)
        return pl.pallas_call(
            body,
            out_shape=[jax.ShapeDtypeStruct(shape, kind) for shape, kind in outs],
            in_specs=specs,
            out_specs=[pl.BlockSpec(memory_space=pltpu.VMEM)] * len(outs),
            scratch_shapes=list(scratch),
            compiler_params=pltpu.CompilerParams(vmem_limit_bytes=LIMIT),
            cost_estimate=pl.CostEstimate(flops=cost * 10**9, bytes_accessed=1000, transcendentals=0),
        )(*operands)

    return run


def staged_call(body, outs, scratch=(), scalars=1, cost=1):
    made = [jax.ShapeDtypeStruct(shape, kind) for shape, kind in outs]

    def run(*operands):
        arrays = operands[scalars:]
        taken, given = len(arrays), len(made)

        def staged(*refs):
            facts, refs = refs[:scalars], refs[scalars:]
            sources, refs = refs[:taken], refs[taken:]
            targets, refs = refs[:given], refs[given:]
            held, refs = refs[:taken], refs[taken:]
            results, refs = refs[:given], refs[given:]
            own, (arrive, leave) = refs[: len(scratch)], refs[len(scratch) :]
            copies = [pltpu.make_async_copy(s, h, arrive.at[i]) for i, (s, h) in enumerate(zip(sources, held))]
            for copy in copies:
                copy.start()
            for copy in copies:
                copy.wait()
            body(*facts, *held, *results, *own)
            copies = [pltpu.make_async_copy(r, t, leave.at[i]) for i, (r, t) in enumerate(zip(results, targets))]
            for copy in copies:
                copy.start()
            for copy in copies:
                copy.wait()

        return pl.pallas_call(
            staged,
            out_shape=made,
            in_specs=[pl.BlockSpec(memory_space=pltpu.SMEM)] * scalars + [pl.BlockSpec(memory_space=pl.ANY)] * taken,
            out_specs=[pl.BlockSpec(memory_space=pl.ANY)] * given,
            scratch_shapes=[pltpu.VMEM(array.shape, array.dtype) for array in (*arrays, *made)]
            + list(scratch)
            + [pltpu.SemaphoreType.DMA((taken,)), pltpu.SemaphoreType.DMA((given,))],
            compiler_params=pltpu.CompilerParams(vmem_limit_bytes=5 * LIMIT),
            cost_estimate=pl.CostEstimate(flops=cost * 10**9, bytes_accessed=1000, transcendentals=0),
        )(*operands)

    return run


def small(body, shape, kind):
    return lambda *operands: call(body, [(shape, kind)], scalars=0)(*operands)[0]


def dot(a, b, dims):
    return lax.dot_general(a, b, (dims, ((), ())), preferred_element_type=F32)


def at(index, size):
    return pl.ds(pl.multiple_of(index * size, size), size)


def valid_rows(start, count, length):
    position = start + lax.broadcasted_iota(jnp.int32, (count, LANES), 0)
    return (position >= 0) & (position < length)


def filter_rows(source, lane, taps, row, count, offsets):
    total = jnp.zeros((count, LANES), F32)
    for phase in range(8):
        chosen = [o for o in offsets if o % 8 == phase]
        reach = max(chosen) - phase
        window = source[row + phase : row + phase + count + reach, lane]
        for o in chosen:
            total = total + window[o - phase : o - phase + count] * taps[offsets[o]][None, :]
    return total


def edge_row(j, low, high, spare):
    return jnp.where(j == 0, low, jnp.where(j == PARTS - 1, high, spare))


def conv_body(facts, first, second, third, fourth, weights, convolved, payload, padded):
    x, z, length, language = facts[0], facts[1], facts[2], facts[3]
    begin = z * FRAMES - TAPS
    for k, piece in enumerate((first, second, third, fourth)):
        j = lax.rem(x - k + PARTS, PARTS)
        main = pl.multiple_of(TAPS + j * OWN, TAPS)
        rim = pl.multiple_of(edge_row(j, 0, TAPS + FRAMES, 2 * TAPS + FRAMES), TAPS)
        for t in range(TILES):
            lane = slice(t * LANES, (t + 1) * LANES)
            keep = valid_rows(begin + main, OWN, length)
            padded[pl.ds(main, OWN), lane] = jnp.where(keep, piece[0:OWN, lane].astype(F32), 0.0)
            keep = valid_rows(begin + rim, TAPS, length)
            padded[pl.ds(rim, TAPS), lane] = jnp.where(keep, piece[OWN : OWN + TAPS, lane].astype(F32), 0.0)
    step = WIDE // 4
    for t in range(TILES):
        lane = slice(t * LANES, (t + 1) * LANES)
        taps = weights[:, pl.ds(pl.multiple_of(x * BLOCK + t * LANES, LANES), LANES)]

        for row in range(0, WIDE, step):
            convolved[row : row + step, lane] = filter_rows(
                padded, lane, taps, row, step, {k: k for k in range(TAPS)}
            )

    count = jnp.clip(length - z * FRAMES, 0, FRAMES).astype(F32)
    keep = valid_rows(z * FRAMES, FRAMES, length)
    lines = []
    spreads = []
    for t in range(TILES):
        lane = slice(t * LANES, (t + 1) * LANES)
        values = convolved[HALF : HALF + FRAMES, lane]
        mean = jnp.sum(jnp.where(keep, values, 0.0), axis=0, keepdims=True) / jnp.maximum(count, 1.0)
        centred = jnp.where(keep, values - mean, 0.0)
        lines.append(mean)
        spreads.append(jnp.sum(centred * centred, axis=0, keepdims=True))
    ones = jnp.ones((1, LANES), F32)
    message = jnp.concatenate(lines + spreads + [ones * language.astype(F32), ones * count], axis=0)
    payload[...] = jnp.broadcast_to(message[None], (MEMBERS, 8, LANES))


def back_body(facts, first, second, third, fourth, own_half, other_half, back, weight):
    x, core = facts[0], facts[4]
    weight[at(core, SHARE), :] = own_half[...]
    weight[at(1 - core, SHARE), :] = other_half[...]
    for k, piece in enumerate((first, second, third, fourth)):
        j = lax.rem(x - k + PARTS, PARTS)
        result = dot(piece[...], weight[...], ((1,), (1,)))
        back[pl.ds(pl.multiple_of(HALF + j * OWN, HALF), OWN), :] = result[0:OWN]
        rim = pl.multiple_of(edge_row(j, 0, HALF + FRAMES, WIDE), HALF)
        back[pl.ds(rim, HALF), :] = result[OWN : OWN + HALF]


def combine(gathered, language):
    same = gathered[:, 6, :] == language.astype(F32)
    counts = jnp.where(same, gathered[:, 7, :], 0.0)
    total = jnp.maximum(jnp.sum(counts, axis=0, keepdims=True), 1.0)
    return same, counts, total


def chosen_row(table, index):
    here = lax.broadcasted_iota(jnp.int32, table.shape, 0) == index
    return jnp.sum(jnp.where(here, table, 0.0), axis=0, keepdims=True)


def act_body(facts, gathered, convolved, back, gains, biases, kept, sent, normed, grad, inverses, payload, active):
    x, z, length, language = facts[0], facts[1], facts[2], facts[3]
    same, counts, total = combine(gathered, language)
    spans = ((0, HALF), (HALF, FRAMES), (HALF + FRAMES, HALF))
    sums = [None] * 8
    sums[6] = sums[7] = jnp.zeros((1, LANES), F32)
    scales = []
    for t in range(TILES):
        lane = slice(t * LANES, (t + 1) * LANES)
        wide_lane = pl.ds(pl.multiple_of(x * BLOCK + t * LANES, LANES), LANES)
        means = gathered[:, t, :]
        average = jnp.sum(means * counts, axis=0, keepdims=True) / total
        spread = jnp.where(same, gathered[:, TILES + t, :], 0.0)
        away = means - average
        variance = jnp.sum(spread + counts * (away * away), axis=0, keepdims=True) / total
        inverse = lax.rsqrt(variance + EPSILON)
        scales.append(inverse)
        gain = chosen_row(gains[:, wide_lane], language)
        bias = chosen_row(biases[:, wide_lane], language)
        for part, (row, size) in enumerate(spans):
            step = min(size, 128)
            first = second = jnp.zeros((1, LANES), F32)
            for at_row in range(0, size, step):
                here = slice(row + at_row, row + at_row + step)
                keep = valid_rows(z * FRAMES - HALF + row + at_row, step, length)
                value = (convolved[here, lane] - average) * inverse
                pre = value * gain + bias
                gate = 1.0 / (1.0 + jnp.exp(-pre))
                upstream = back[here, lane]
                slope = jnp.where(keep, upstream * gate * (1.0 + pre * (1.0 - gate)), 0.0) * gain
                normed[here, lane] = value
                grad[here, lane] = slope
                if part == 1:
                    active[at_row : at_row + step, lane] = jnp.where(keep, pre * gate, 0.0).astype(BF16)
                    first = first + jnp.sum(slope, axis=0, keepdims=True)
                    second = second + jnp.sum(slope * value, axis=0, keepdims=True)
            if part == 1:
                sums[t], sums[TILES + t] = first, second
    payload[...] = jnp.broadcast_to(jnp.concatenate(sums, axis=0)[None], (MEMBERS, 8, LANES))
    first_core = facts[4] == 0
    kept[...] = jnp.where(first_core, active[:, :SHARE], active[:, SHARE:])
    sent[...] = jnp.where(first_core, active[:, SHARE:], active[:, :SHARE])
    inverses[...] = jnp.concatenate(scales + [sums[6]] * (8 - TILES), axis=0)


def grad_body(facts, gathered, sums, normed, grad, inverses, weights, first, second, third, fourth, rounded, result):
    x, z, length, language = facts[0], facts[1], facts[2], facts[3]
    same, counts, total = combine(gathered, language)
    keep = valid_rows(z * FRAMES - HALF, WIDE, length)
    step = FRAMES // 4
    for t in range(TILES):
        lane = slice(t * LANES, (t + 1) * LANES)
        shift = jnp.sum(jnp.where(same, sums[:, t, :], 0.0), axis=0, keepdims=True) / total
        scale = jnp.sum(jnp.where(same, sums[:, TILES + t, :], 0.0), axis=0, keepdims=True) / total
        inverse = inverses[t : t + 1, :]
        value = inverse * (grad[:, lane] - shift - normed[:, lane] * scale)
        rounded[:, lane] = jnp.where(keep, value, 0.0).astype(BF16).astype(F32)
    for t in range(TILES):
        lane = slice(t * LANES, (t + 1) * LANES)
        taps = weights[:, pl.ds(pl.multiple_of(x * BLOCK + t * LANES, LANES), LANES)]

        for row in range(0, FRAMES, step):
            value = filter_rows(rounded, lane, taps, row, step, {TAPS - k: k for k in range(TAPS)})
            inside = valid_rows(z * FRAMES + row, step, length)
            result[row : row + step, lane] = jnp.where(inside, value, 0.0)

    for k, piece in enumerate((first, second, third, fourth)):
        j = lax.rem(x + k, PARTS)
        piece[...] = result[at(j, OWN), :].astype(BF16)


def lanes_body(facts, first, second, third, fourth, joined):
    x = facts[0]
    for k, piece in enumerate((first, second, third, fourth)):
        j = lax.rem(x - k + PARTS, PARTS)
        joined[:, pl.ds(pl.multiple_of(j * BLOCK, LANES), BLOCK)] = piece[...]


def out_body(facts, mine, theirs, own_half, other_half, kept, first, second, third):
    x = facts[0]
    for k, piece in enumerate((kept, first, second, third)):
        rows = at(lax.rem(x + k, PARTS), OWN)
        total = dot(mine[rows, :], own_half[...], ((1,), (0,))) + dot(theirs[rows, :], other_half[...], ((1,), (0,)))
        piece[...] = total.astype(piece.dtype)


def product_body(facts, mine, theirs, first, second, third, fourth, kept, *sent):
    x = facts[0]
    for half in (theirs, mine):
        total = jnp.zeros((SHARE, CHANNELS), F32)
        for k, piece in enumerate((first, second, third, fourth)):
            j = lax.rem(x - k + PARTS, PARTS)
            total = total + dot(half[at(j, OWN), :], piece[0:OWN, :], ((0,), (0,)))
        if half is mine:
            kept[...] = total
        else:
            for n, target in enumerate(sent):
                target[...] = total[n * STRIP : (n + 1) * STRIP].astype(BF16)


def slots(q):
    row = lax.broadcasted_iota(jnp.int32, (SENT, 1), 0)
    inner = lax.rem(row, SLOT)
    wanted = jnp.where(inner // ROWS == q, row // SLOT * ROWS + lax.rem(inner, ROWS), -1)
    return (lax.broadcasted_iota(jnp.int32, (SENT, SHARE), 1) == wanted).astype(BF16)


def tile_at(q, g):
    start = (FOLD * g + q) * LANES
    return slice(start, start + LANES)


def folded(block, q):
    return jnp.concatenate([block[:, tile_at(q, g)] for g in range(TILES)], axis=1)


def copies_body(row_block, copies):
    inner = lax.rem(lax.broadcasted_iota(jnp.int32, (SENT, ROWS), 0), SLOT)
    column = lax.broadcasted_iota(jnp.int32, (SENT, ROWS), 1)
    total = jnp.zeros((SENT, BLOCK), F32)
    for q in range(FOLD):
        choose = (inner == q * ROWS + column).astype(BF16)
        total = total + dot(choose, folded(row_block[...], q), ((1,), (0,)))
    copies[...] = total.astype(BF16)


def weight_body(rows, half):
    for q in range(FOLD):
        part = dot(slots(q), rows[...], ((0,), (0,))).astype(BF16)
        for g in range(TILES):
            half[:, tile_at(q, g)] = part[:, g * LANES : (g + 1) * LANES]


def spread_body(kept, first, second, third, fourth, spread):
    other = jnp.concatenate([strip[...].astype(F32) for strip in (first, second, third, fourth)], axis=0)
    both = (kept[...] + other).astype(BF16)
    total = jnp.zeros((SENT, BLOCK), F32)
    for q in range(FOLD):
        total = total + dot(slots(q), folded(both, q), ((1,), (0,)))
    spread[...] = total.astype(BF16)


def unfold_body(sums, rows):
    for q in range(FOLD):
        for g in range(TILES):
            rows[:, tile_at(q, g)] = sums[q * ROWS : (q + 1) * ROWS, g * LANES : (g + 1) * LANES]


def around_x(piece, shift):
    size = AXES["x"]
    return lax.ppermute(piece, "x", [(i, (i + shift) % size) for i in range(size)])


def other_core(block):
    return lax.ppermute(block, "c", [(0, 1), (1, 0)])


def swap_xy(block):
    pairs = [(y * 4 + x, x * 4 + y) for y in range(4) for x in range(4)]
    return lax.ppermute(block, ("y", "x"), pairs)


def wait_for(value, *others):
    return lax.optimization_barrier((value,) + others)[0]


def between_blocks(rows):
    ends = [(4 * z + 3, 4 * z + 4) for z in range(AXES["z"] - 1)]
    return lax.ppermute(rows, ("z", "x"), ends + [(b, a) for a, b in ends])


def exchange(payload, axes):
    return lax.all_to_all(payload, axes, 0, 0, tiled=True)


def on_device(glu_out, conv_weight, bn_gain, bn_bias, w_out, cotangent, language, length):
    glu, cot = glu_out[0], cotangent[0]
    x, y, z, core = (lax.axis_index(axis) for axis in ("x", "y", "z", "c"))
    facts = jnp.stack([x, z, length[0], language[0], core, y]).astype(jnp.int32)

    last = x == PARTS - 1
    rim = jnp.concatenate(
        [
            lax.dynamic_slice_in_dim(glu, jnp.where(last, OWN - TAPS, 0), TAPS, 0),
            lax.dynamic_slice_in_dim(cot, jnp.where(last, OWN - HALF, 0), HALF, 0),
        ],
        axis=0,
    )
    rim = between_blocks(rim)
    copies = small(copies_body, (SENT, BLOCK), BF16)(swap_xy(w_out))

    pieces = []
    for k in range(PARTS):
        column = lax.rem(x + k, PARTS) * BLOCK
        own = lax.dynamic_slice(glu, (0, column), (OWN, BLOCK))
        piece = jnp.concatenate([own, lax.dynamic_slice(rim, (0, column), (TAPS, BLOCK))], axis=0)
        pieces.append(around_x(piece, k) if k else piece)
    rows = exchange(wait_for(copies, *pieces), ("z", "y"))
    cot = wait_for(jnp.concatenate([cot, rim[TAPS:]], axis=0), *pieces)
    cots = [cot] + [around_x(cot, k) for k in range(1, PARTS)]
    convolved, payload = call(
        conv_body,
        [((WIDE, BLOCK), F32), ((MEMBERS, 8, LANES), F32)],
        [pltpu.VMEM((FRAMES + 3 * TAPS, BLOCK), F32)],
        cost=5,
    )(facts, *pieces, conv_weight)

    (half,) = call(weight_body, [((SHARE, CHANNELS), BF16)], scalars=0)(wait_for(rows, payload))
    gathered = exchange(wait_for(payload, *cots), STATS)
    other_half = other_core(half)
    (back,) = call(back_body, [((WIDE + HALF, BLOCK), F32)], [pltpu.VMEM((BLOCK, CHANNELS), BF16)], cost=3)(
        facts, *cots, half, other_half
    )

    kept, sent, normed, grad, inverses, payload = staged_call(
        act_body,
        [
            ((FRAMES, SHARE), BF16),
            ((FRAMES, SHARE), BF16),
            ((WIDE, BLOCK), F32),
            ((WIDE, BLOCK), F32),
            ((8, LANES), F32),
            ((MEMBERS, 8, LANES), F32),
        ],
        [pltpu.VMEM((FRAMES, BLOCK), BF16)],
        cost=2,
    )(facts, gathered, convolved, back, bn_gain, bn_bias)
    sums = exchange(payload, STATS)

    output, *others = call(out_body, [((OWN, CHANNELS), F32)] + [((OWN, CHANNELS), BF16)] * (PARTS - 1))(
        facts, kept, sent, half, other_half
    )
    arrived = [around_x(piece, k + 1) for k, piece in enumerate(others)]

    kept, *sent = call(product_body, [((SHARE, CHANNELS), F32)] + [((STRIP, CHANNELS), BF16)] * 4)(
        facts, wait_for(kept, *others), sent, *cots
    )
    (spread,) = call(spread_body, [((SENT, BLOCK), BF16)], scalars=0)(kept, *[other_core(strip) for strip in sent])
    spread = exchange(spread, ("z", "y")).reshape(32, SLOT, BLOCK)
    spread = swap_xy(jnp.sum(spread.astype(F32), axis=0))
    (weight_grad,) = call(unfold_body, [((ROWS, CHANNELS), F32)], scalars=0)(spread)

    pieces = call(
        grad_body,
        [((OWN, BLOCK), BF16)] * PARTS,
        [pltpu.VMEM((WIDE, BLOCK), F32), pltpu.VMEM((FRAMES, BLOCK), F32)],
        cost=5,
    )(facts, gathered, wait_for(sums, *arrived), normed, grad, inverses, conv_weight)
    for piece in arrived:
        output = output + wait_for(piece, *pieces).astype(F32)
    output = output.astype(BF16)
    pieces = [pieces[0]] + [around_x(pieces[k], k) for k in range(1, PARTS)]
    (input_grad,) = call(lanes_body, [((OWN, CHANNELS), BF16)])(facts, *pieces)
    return output[None], weight_grad, input_grad[None]


def solution(mesh):
    fine = Mesh(mesh.devices.reshape(tuple(AXES.values())), tuple(AXES))
    dp, seq = ("y", "c"), ("z", "x")
    placed = (
        P(dp, seq, None),
        P(),
        P(),
        P(),
        P(dp + seq, None),
        P(dp, seq, None),
        P(dp),
        P(dp),
    )
    return jax.shard_map(
        on_device,
        mesh=fine,
        in_specs=placed,
        out_specs=(P(dp, seq, None), P(dp + seq, None), P(dp, seq, None)),
        check_vma=False,
    )
```

```python
import jax
import jax.numpy as jnp
from jax import lax
from jax.experimental import pallas as pl
from jax.experimental.pallas import tpu as pltpu
from jax.sharding import Mesh, PartitionSpec as P

EPSILON = 1e-05
F32 = jnp.float32
BF16 = jnp.bfloat16
AXES = {"y": 4, "c": 2, "z": 8, "x": 4}
STATS = ("c", "z", "y")
MEMBERS = 64
LANES = 128
PARTS = 4
OWN = 128
FRAMES = 512
BLOCK = 384
TILES = BLOCK // LANES
CHANNELS = 1536
TAPS = 32
HALF = 16
WIDE = FRAMES + 2 * HALF
ROWS = 6
FOLD = 4
SLOT = FOLD * ROWS
SENT = 32 * SLOT
SHARE = 192
STRIP = SHARE // 4
LIMIT = 12 * 1024 * 1024


def call(body, outs, scratch=(), scalars=1, cost=1):
    def run(*operands):
        specs = [pl.BlockSpec(memory_space=pltpu.SMEM)] * scalars
        specs += [pl.BlockSpec(memory_space=pltpu.VMEM)] * (len(operands) - scalars)
        return pl.pallas_call(
            body,
            out_shape=[jax.ShapeDtypeStruct(shape, kind) for shape, kind in outs],
            in_specs=specs,
            out_specs=[pl.BlockSpec(memory_space=pltpu.VMEM)] * len(outs),
            scratch_shapes=list(scratch),
            compiler_params=pltpu.CompilerParams(vmem_limit_bytes=LIMIT),
            cost_estimate=pl.CostEstimate(flops=cost * 10**9, bytes_accessed=1000, transcendentals=0),
        )(*operands)

    return run


def staged_call(body, outs, scratch=(), scalars=1, cost=1):
    made = [jax.ShapeDtypeStruct(shape, kind) for shape, kind in outs]

    def run(*operands):
        arrays = operands[scalars:]
        taken, given = len(arrays), len(made)

        def staged(*refs):
            facts, refs = refs[:scalars], refs[scalars:]
            sources, refs = refs[:taken], refs[taken:]
            targets, refs = refs[:given], refs[given:]
            held, refs = refs[:taken], refs[taken:]
            results, refs = refs[:given], refs[given:]
            own, (arrive, leave) = refs[: len(scratch)], refs[len(scratch) :]
            copies = [pltpu.make_async_copy(s, h, arrive.at[i]) for i, (s, h) in enumerate(zip(sources, held))]
            for copy in copies:
                copy.start()
            for copy in copies:
                copy.wait()
            body(*facts, *held, *results, *own)
            copies = [pltpu.make_async_copy(r, t, leave.at[i]) for i, (r, t) in enumerate(zip(results, targets))]
            for copy in copies:
                copy.start()
            for copy in copies:
                copy.wait()

        return pl.pallas_call(
            staged,
            out_shape=made,
            in_specs=[pl.BlockSpec(memory_space=pltpu.SMEM)] * scalars + [pl.BlockSpec(memory_space=pl.ANY)] * taken,
            out_specs=[pl.BlockSpec(memory_space=pl.ANY)] * given,
            scratch_shapes=[pltpu.VMEM(array.shape, array.dtype) for array in (*arrays, *made)]
            + list(scratch)
            + [pltpu.SemaphoreType.DMA((taken,)), pltpu.SemaphoreType.DMA((given,))],
            compiler_params=pltpu.CompilerParams(vmem_limit_bytes=5 * LIMIT),
            cost_estimate=pl.CostEstimate(flops=cost * 10**9, bytes_accessed=1000, transcendentals=0),
        )(*operands)

    return run


def small(body, shape, kind):
    return lambda *operands: call(body, [(shape, kind)], scalars=0)(*operands)[0]


def dot(a, b, dims):
    return lax.dot_general(a, b, (dims, ((), ())), preferred_element_type=F32)


def at(index, size):
    return pl.ds(pl.multiple_of(index * size, size), size)


def valid_rows(start, count, length):
    position = start + lax.broadcasted_iota(jnp.int32, (count, LANES), 0)
    return (position >= 0) & (position < length)


def filter_rows(source, lane, taps, row, count, offsets):
    total = jnp.zeros((count, LANES), F32)
    for phase in range(8):
        chosen = [o for o in offsets if o % 8 == phase]
        reach = max(chosen) - phase
        window = source[row + phase : row + phase + count + reach, lane]
        for o in chosen:
            total = total + window[o - phase : o - phase + count] * taps[offsets[o]][None, :]
    return total


def edge_row(j, low, high, spare):
    return jnp.where(j == 0, low, jnp.where(j == PARTS - 1, high, spare))


def conv_body(facts, first, second, third, fourth, weights, convolved, payload, padded):
    x, z, length, language = facts[0], facts[1], facts[2], facts[3]
    begin = z * FRAMES - TAPS
    for k, piece in enumerate((first, second, third, fourth)):
        j = lax.rem(x - k + PARTS, PARTS)
        main = pl.multiple_of(TAPS + j * OWN, TAPS)
        rim = pl.multiple_of(edge_row(j, 0, TAPS + FRAMES, 2 * TAPS + FRAMES), TAPS)
        for t in range(TILES):
            lane = slice(t * LANES, (t + 1) * LANES)
            keep = valid_rows(begin + main, OWN, length)
            padded[pl.ds(main, OWN), lane] = jnp.where(keep, piece[0:OWN, lane].astype(F32), 0.0)
            keep = valid_rows(begin + rim, TAPS, length)
            padded[pl.ds(rim, TAPS), lane] = jnp.where(keep, piece[OWN : OWN + TAPS, lane].astype(F32), 0.0)
    step = WIDE // 4
    for t in range(TILES):
        lane = slice(t * LANES, (t + 1) * LANES)
        taps = weights[:, pl.ds(pl.multiple_of(x * BLOCK + t * LANES, LANES), LANES)]

        for row in range(0, WIDE, step):
            convolved[row : row + step, lane] = filter_rows(
                padded, lane, taps, row, step, {k: k for k in range(TAPS)}
            )

    count = jnp.clip(length - z * FRAMES, 0, FRAMES).astype(F32)
    keep = valid_rows(z * FRAMES, FRAMES, length)
    lines = []
    spreads = []
    for t in range(TILES):
        lane = slice(t * LANES, (t + 1) * LANES)
        values = convolved[HALF : HALF + FRAMES, lane]
        mean = jnp.sum(jnp.where(keep, values, 0.0), axis=0, keepdims=True) / jnp.maximum(count, 1.0)
        centred = jnp.where(keep, values - mean, 0.0)
        lines.append(mean)
        spreads.append(jnp.sum(centred * centred, axis=0, keepdims=True))
    ones = jnp.ones((1, LANES), F32)
    message = jnp.concatenate(lines + spreads + [ones * language.astype(F32), ones * count], axis=0)
    payload[...] = jnp.broadcast_to(message[None], (MEMBERS, 8, LANES))


def back_body(facts, first, second, third, fourth, own_half, other_half, back, weight):
    x, core = facts[0], facts[4]
    weight[at(core, SHARE), :] = own_half[...]
    weight[at(1 - core, SHARE), :] = other_half[...]
    for k, piece in enumerate((first, second, third, fourth)):
        j = lax.rem(x - k + PARTS, PARTS)
        result = dot(piece[...], weight[...], ((1,), (1,)))
        back[pl.ds(pl.multiple_of(HALF + j * OWN, HALF), OWN), :] = result[0:OWN]
        rim = pl.multiple_of(edge_row(j, 0, HALF + FRAMES, WIDE), HALF)
        back[pl.ds(rim, HALF), :] = result[OWN : OWN + HALF]


def combine(gathered, language):
    same = gathered[:, 6, :] == language.astype(F32)
    counts = jnp.where(same, gathered[:, 7, :], 0.0)
    total = jnp.maximum(jnp.sum(counts, axis=0, keepdims=True), 1.0)
    return same, counts, total


def chosen_row(table, index):
    here = lax.broadcasted_iota(jnp.int32, table.shape, 0) == index
    return jnp.sum(jnp.where(here, table, 0.0), axis=0, keepdims=True)


def act_body(facts, gathered, convolved, back, gains, biases, kept, sent, normed, grad, inverses, payload, active):
    x, z, length, language = facts[0], facts[1], facts[2], facts[3]
    same, counts, total = combine(gathered, language)
    spans = ((0, HALF), (HALF, FRAMES), (HALF + FRAMES, HALF))
    sums = [None] * 8
    sums[6] = sums[7] = jnp.zeros((1, LANES), F32)
    scales = []
    for t in range(TILES):
        lane = slice(t * LANES, (t + 1) * LANES)
        wide_lane = pl.ds(pl.multiple_of(x * BLOCK + t * LANES, LANES), LANES)
        means = gathered[:, t, :]
        average = jnp.sum(means * counts, axis=0, keepdims=True) / total
        spread = jnp.where(same, gathered[:, TILES + t, :], 0.0)
        away = means - average
        variance = jnp.sum(spread + counts * (away * away), axis=0, keepdims=True) / total
        inverse = lax.rsqrt(variance + EPSILON)
        scales.append(inverse)
        gain = chosen_row(gains[:, wide_lane], language)
        bias = chosen_row(biases[:, wide_lane], language)
        for part, (row, size) in enumerate(spans):
            step = min(size, 128)
            first = second = jnp.zeros((1, LANES), F32)
            for at_row in range(0, size, step):
                here = slice(row + at_row, row + at_row + step)
                keep = valid_rows(z * FRAMES - HALF + row + at_row, step, length)
                value = (convolved[here, lane] - average) * inverse
                pre = value * gain + bias
                gate = 1.0 / (1.0 + jnp.exp(-pre))
                upstream = back[here, lane]
                slope = jnp.where(keep, upstream * gate * (1.0 + pre * (1.0 - gate)), 0.0) * gain
                normed[here, lane] = value
                grad[here, lane] = slope
                if part == 1:
                    active[at_row : at_row + step, lane] = jnp.where(keep, pre * gate, 0.0).astype(BF16)
                    first = first + jnp.sum(slope, axis=0, keepdims=True)
                    second = second + jnp.sum(slope * value, axis=0, keepdims=True)
            if part == 1:
                sums[t], sums[TILES + t] = first, second
    payload[...] = jnp.broadcast_to(jnp.concatenate(sums, axis=0)[None], (MEMBERS, 8, LANES))
    first_core = facts[4] == 0
    kept[...] = jnp.where(first_core, active[:, :SHARE], active[:, SHARE:])
    sent[...] = jnp.where(first_core, active[:, SHARE:], active[:, :SHARE])
    inverses[...] = jnp.concatenate(scales + [sums[6]] * (8 - TILES), axis=0)


def grad_body(facts, gathered, sums, normed, grad, inverses, weights, first, second, third, fourth, rounded, result):
    x, z, length, language = facts[0], facts[1], facts[2], facts[3]
    same, counts, total = combine(gathered, language)
    keep = valid_rows(z * FRAMES - HALF, WIDE, length)
    step = FRAMES // 4
    for t in range(TILES):
        lane = slice(t * LANES, (t + 1) * LANES)
        shift = jnp.sum(jnp.where(same, sums[:, t, :], 0.0), axis=0, keepdims=True) / total
        scale = jnp.sum(jnp.where(same, sums[:, TILES + t, :], 0.0), axis=0, keepdims=True) / total
        inverse = inverses[t : t + 1, :]
        value = inverse * (grad[:, lane] - shift - normed[:, lane] * scale)
        rounded[:, lane] = jnp.where(keep, value, 0.0).astype(BF16).astype(F32)
    for t in range(TILES):
        lane = slice(t * LANES, (t + 1) * LANES)
        taps = weights[:, pl.ds(pl.multiple_of(x * BLOCK + t * LANES, LANES), LANES)]

        for row in range(0, FRAMES, step):
            value = filter_rows(rounded, lane, taps, row, step, {TAPS - k: k for k in range(TAPS)})
            inside = valid_rows(z * FRAMES + row, step, length)
            result[row : row + step, lane] = jnp.where(inside, value, 0.0)

    for k, piece in enumerate((first, second, third, fourth)):
        j = lax.rem(x + k, PARTS)
        piece[...] = result[at(j, OWN), :].astype(BF16)


def lanes_body(facts, first, second, third, fourth, joined):
    x = facts[0]
    for k, piece in enumerate((first, second, third, fourth)):
        j = lax.rem(x - k + PARTS, PARTS)
        joined[:, pl.ds(pl.multiple_of(j * BLOCK, LANES), BLOCK)] = piece[...]


def out_body(facts, mine, theirs, own_half, other_half, kept, first, second, third):
    x = facts[0]
    for k, piece in enumerate((kept, first, second, third)):
        rows = at(lax.rem(x + k, PARTS), OWN)
        total = dot(mine[rows, :], own_half[...], ((1,), (0,))) + dot(theirs[rows, :], other_half[...], ((1,), (0,)))
        piece[...] = total.astype(piece.dtype)


def product_body(facts, mine, theirs, first, second, third, fourth, kept, *sent):
    x = facts[0]
    for half in (theirs, mine):
        total = jnp.zeros((SHARE, CHANNELS), F32)
        for k, piece in enumerate((first, second, third, fourth)):
            j = lax.rem(x - k + PARTS, PARTS)
            total = total + dot(half[at(j, OWN), :], piece[0:OWN, :], ((0,), (0,)))
        if half is mine:
            kept[...] = total
        else:
            for n, target in enumerate(sent):
                target[...] = total[n * STRIP : (n + 1) * STRIP].astype(BF16)


def slots(q):
    row = lax.broadcasted_iota(jnp.int32, (SENT, 1), 0)
    inner = lax.rem(row, SLOT)
    wanted = jnp.where(inner // ROWS == q, row // SLOT * ROWS + lax.rem(inner, ROWS), -1)
    return (lax.broadcasted_iota(jnp.int32, (SENT, SHARE), 1) == wanted).astype(BF16)


def tile_at(q, g):
    start = (FOLD * g + q) * LANES
    return slice(start, start + LANES)


def folded(block, q):
    return jnp.concatenate([block[:, tile_at(q, g)] for g in range(TILES)], axis=1)


def copies_body(row_block, copies):
    inner = lax.rem(lax.broadcasted_iota(jnp.int32, (SENT, ROWS), 0), SLOT)
    column = lax.broadcasted_iota(jnp.int32, (SENT, ROWS), 1)
    total = jnp.zeros((SENT, BLOCK), F32)
    for q in range(FOLD):
        choose = (inner == q * ROWS + column).astype(BF16)
        total = total + dot(choose, folded(row_block[...], q), ((1,), (0,)))
    copies[...] = total.astype(BF16)


def weight_body(rows, half):
    for q in range(FOLD):
        part = dot(slots(q), rows[...], ((0,), (0,))).astype(BF16)
        for g in range(TILES):
            half[:, tile_at(q, g)] = part[:, g * LANES : (g + 1) * LANES]


def spread_body(kept, first, second, third, fourth, spread):
    other = jnp.concatenate([strip[...].astype(F32) for strip in (first, second, third, fourth)], axis=0)
    both = (kept[...] + other).astype(BF16)
    total = jnp.zeros((SENT, BLOCK), F32)
    for q in range(FOLD):
        total = total + dot(slots(q), folded(both, q), ((1,), (0,)))
    spread[...] = total.astype(BF16)


def unfold_body(sums, rows):
    for q in range(FOLD):
        for g in range(TILES):
            rows[:, tile_at(q, g)] = sums[q * ROWS : (q + 1) * ROWS, g * LANES : (g + 1) * LANES]


def around_x(piece, shift):
    size = AXES["x"]
    return lax.ppermute(piece, "x", [(i, (i + shift) % size) for i in range(size)])


def other_core(block):
    return lax.ppermute(block, "c", [(0, 1), (1, 0)])


def swap_xy(block):
    pairs = [(y * 4 + x, x * 4 + y) for y in range(4) for x in range(4)]
    return lax.ppermute(block, ("y", "x"), pairs)


def wait_for(value, *others):
    return lax.optimization_barrier((value,) + others)[0]


def between_blocks(rows):
    ends = [(4 * z + 3, 4 * z + 4) for z in range(AXES["z"] - 1)]
    return lax.ppermute(rows, ("z", "x"), ends + [(b, a) for a, b in ends])


def exchange(payload, axes):
    return lax.all_to_all(payload, axes, 0, 0, tiled=True)


def on_device(glu_out, conv_weight, bn_gain, bn_bias, w_out, cotangent, language, length):
    glu, cot = glu_out[0], cotangent[0]
    x, y, z, core = (lax.axis_index(axis) for axis in ("x", "y", "z", "c"))
    facts = jnp.stack([x, z, length[0], language[0], core, y]).astype(jnp.int32)

    last = x == PARTS - 1
    rim = jnp.concatenate(
        [
            lax.dynamic_slice_in_dim(glu, jnp.where(last, OWN - TAPS, 0), TAPS, 0),
            lax.dynamic_slice_in_dim(cot, jnp.where(last, OWN - HALF, 0), HALF, 0),
        ],
        axis=0,
    )
    rim = between_blocks(rim)
    copies = small(copies_body, (SENT, BLOCK), BF16)(swap_xy(w_out))

    pieces = []
    for k in range(PARTS):
        column = lax.rem(x + k, PARTS) * BLOCK
        own = lax.dynamic_slice(glu, (0, column), (OWN, BLOCK))
        piece = jnp.concatenate([own, lax.dynamic_slice(rim, (0, column), (TAPS, BLOCK))], axis=0)
        pieces.append(around_x(piece, k) if k else piece)
    rows = exchange(wait_for(copies, *pieces), ("z", "y"))
    cot = wait_for(jnp.concatenate([cot, rim[TAPS:]], axis=0), *pieces)
    cots = [cot] + [around_x(cot, k) for k in range(1, PARTS)]
    convolved, payload = call(
        conv_body,
        [((WIDE, BLOCK), F32), ((MEMBERS, 8, LANES), F32)],
        [pltpu.VMEM((FRAMES + 3 * TAPS, BLOCK), F32)],
        cost=5,
    )(facts, *pieces, conv_weight)

    (half,) = call(weight_body, [((SHARE, CHANNELS), BF16)], scalars=0)(wait_for(rows, payload))
    gathered = exchange(wait_for(payload, *cots), STATS)
    other_half = other_core(half)
    (back,) = call(back_body, [((WIDE + HALF, BLOCK), F32)], [pltpu.VMEM((BLOCK, CHANNELS), BF16)], cost=3)(
        facts, *cots, half, other_half
    )

    kept, sent, normed, grad, inverses, payload = staged_call(
        act_body,
        [
            ((FRAMES, SHARE), BF16),
            ((FRAMES, SHARE), BF16),
            ((WIDE, BLOCK), F32),
            ((WIDE, BLOCK), F32),
            ((8, LANES), F32),
            ((MEMBERS, 8, LANES), F32),
        ],
        [pltpu.VMEM((FRAMES, BLOCK), BF16)],
        cost=2,
    )(facts, gathered, convolved, back, bn_gain, bn_bias)
    sums = exchange(payload, STATS)

    output, *others = call(out_body, [((OWN, CHANNELS), F32)] + [((OWN, CHANNELS), BF16)] * (PARTS - 1), cost=1)(
        facts, kept, sent, half, other_half
    )
    arrived = [around_x(piece, k + 1) for k, piece in enumerate(others)]

    kept, *sent = call(product_body, [((SHARE, CHANNELS), F32)] + [((STRIP, CHANNELS), BF16)] * 4)(
        facts, wait_for(kept, *others), sent, *cots
    )
    (spread,) = call(spread_body, [((SENT, BLOCK), BF16)], scalars=0)(kept, *[other_core(strip) for strip in sent])
    spread = exchange(spread, ("z", "y")).reshape(32, SLOT, BLOCK)
    spread = swap_xy(jnp.sum(spread.astype(F32), axis=0))
    (weight_grad,) = call(unfold_body, [((ROWS, CHANNELS), F32)], scalars=0)(spread)

    pieces = call(
        grad_body,
        [((OWN, BLOCK), BF16)] * PARTS,
        [pltpu.VMEM((WIDE, BLOCK), F32), pltpu.VMEM((FRAMES, BLOCK), F32)],
        cost=12,
    )(facts, gathered, wait_for(sums, *arrived), normed, grad, inverses, conv_weight)
    pieces = [pieces[0]] + [around_x(pieces[k], k) for k in range(1, PARTS)]
    (input_grad,) = call(lanes_body, [((OWN, CHANNELS), BF16)])(facts, *pieces)
    for piece in arrived:
        output = output + wait_for(piece, input_grad).astype(F32)
    output = output.astype(BF16)
    return output[None], weight_grad, input_grad[None]


def solution(mesh):
    fine = Mesh(mesh.devices.reshape(tuple(AXES.values())), tuple(AXES))
    dp, seq = ("y", "c"), ("z", "x")
    placed = (
        P(dp, seq, None),
        P(),
        P(),
        P(),
        P(dp + seq, None),
        P(dp, seq, None),
        P(dp),
        P(dp),
    )
    return jax.shard_map(
        on_device,
        mesh=fine,
        in_specs=placed,
        out_specs=(P(dp, seq, None), P(dp + seq, None), P(dp, seq, None)),
        check_vma=False,
    )
```

```python
import jax
import jax.numpy as jnp
from jax import lax
from jax.experimental import pallas as pl
from jax.experimental.pallas import tpu as pltpu
from jax.sharding import Mesh, PartitionSpec as P

EPSILON = 1e-05
F32 = jnp.float32
BF16 = jnp.bfloat16
AXES = {"y": 4, "c": 2, "z": 8, "x": 4}
STATS = ("c", "z", "y")
MEMBERS = 64
LANES = 128
PARTS = 4
OWN = 128
FRAMES = 512
BLOCK = 384
TILES = BLOCK // LANES
CHANNELS = 1536
TAPS = 32
HALF = 16
WIDE = FRAMES + 2 * HALF
ROWS = 6
FOLD = 4
SLOT = FOLD * ROWS
SENT = 32 * SLOT
SHARE = 192
STRIP = SHARE // 4
LIMIT = 12 * 1024 * 1024


def call(body, outs, scratch=(), scalars=1, cost=1):
    def run(*operands):
        specs = [pl.BlockSpec(memory_space=pltpu.SMEM)] * scalars
        specs += [pl.BlockSpec(memory_space=pltpu.VMEM)] * (len(operands) - scalars)
        return pl.pallas_call(
            body,
            out_shape=[jax.ShapeDtypeStruct(shape, kind) for shape, kind in outs],
            in_specs=specs,
            out_specs=[pl.BlockSpec(memory_space=pltpu.VMEM)] * len(outs),
            scratch_shapes=list(scratch),
            compiler_params=pltpu.CompilerParams(vmem_limit_bytes=LIMIT),
            cost_estimate=pl.CostEstimate(flops=cost * 10**9, bytes_accessed=1000, transcendentals=0),
        )(*operands)

    return run


def staged_call(body, outs, scratch=(), scalars=1, cost=1):
    made = [jax.ShapeDtypeStruct(shape, kind) for shape, kind in outs]

    def run(*operands):
        arrays = operands[scalars:]
        taken, given = len(arrays), len(made)

        def staged(*refs):
            facts, refs = refs[:scalars], refs[scalars:]
            sources, refs = refs[:taken], refs[taken:]
            targets, refs = refs[:given], refs[given:]
            held, refs = refs[:taken], refs[taken:]
            results, refs = refs[:given], refs[given:]
            own, (arrive, leave) = refs[: len(scratch)], refs[len(scratch) :]
            copies = [pltpu.make_async_copy(s, h, arrive.at[i]) for i, (s, h) in enumerate(zip(sources, held))]
            for copy in copies:
                copy.start()
            for copy in copies:
                copy.wait()
            body(*facts, *held, *results, *own)
            copies = [pltpu.make_async_copy(r, t, leave.at[i]) for i, (r, t) in enumerate(zip(results, targets))]
            for copy in copies:
                copy.start()
            for copy in copies:
                copy.wait()

        return pl.pallas_call(
            staged,
            out_shape=made,
            in_specs=[pl.BlockSpec(memory_space=pltpu.SMEM)] * scalars + [pl.BlockSpec(memory_space=pl.ANY)] * taken,
            out_specs=[pl.BlockSpec(memory_space=pl.ANY)] * given,
            scratch_shapes=[pltpu.VMEM(array.shape, array.dtype) for array in (*arrays, *made)]
            + list(scratch)
            + [pltpu.SemaphoreType.DMA((taken,)), pltpu.SemaphoreType.DMA((given,))],
            compiler_params=pltpu.CompilerParams(vmem_limit_bytes=5 * LIMIT),
            cost_estimate=pl.CostEstimate(flops=cost * 10**9, bytes_accessed=1000, transcendentals=0),
        )(*operands)

    return run


def small(body, shape, kind):
    return lambda *operands: call(body, [(shape, kind)], scalars=0)(*operands)[0]


def dot(a, b, dims):
    return lax.dot_general(a, b, (dims, ((), ())), preferred_element_type=F32)


def at(index, size):
    return pl.ds(pl.multiple_of(index * size, size), size)


def valid_rows(start, count, length):
    position = start + lax.broadcasted_iota(jnp.int32, (count, LANES), 0)
    return (position >= 0) & (position < length)


def filter_rows(source, lane, taps, row, count, offsets):
    total = jnp.zeros((count, LANES), F32)
    for phase in range(8):
        chosen = [o for o in offsets if o % 8 == phase]
        reach = max(chosen) - phase
        window = source[row + phase : row + phase + count + reach, lane]
        for o in chosen:
            total = total + window[o - phase : o - phase + count] * taps[offsets[o]][None, :]
    return total


def edge_row(j, low, high, spare):
    return jnp.where(j == 0, low, jnp.where(j == PARTS - 1, high, spare))


def conv_body(facts, first, second, third, fourth, weights, convolved, payload, padded):
    x, z, length, language = facts[0], facts[1], facts[2], facts[3]
    begin = z * FRAMES - TAPS
    for k, piece in enumerate((first, second, third, fourth)):
        j = lax.rem(x - k + PARTS, PARTS)
        main = pl.multiple_of(TAPS + j * OWN, TAPS)
        rim = pl.multiple_of(edge_row(j, 0, TAPS + FRAMES, 2 * TAPS + FRAMES), TAPS)
        for t in range(TILES):
            lane = slice(t * LANES, (t + 1) * LANES)
            keep = valid_rows(begin + main, OWN, length)
            padded[pl.ds(main, OWN), lane] = jnp.where(keep, piece[0:OWN, lane].astype(F32), 0.0)
            keep = valid_rows(begin + rim, TAPS, length)
            padded[pl.ds(rim, TAPS), lane] = jnp.where(keep, piece[OWN : OWN + TAPS, lane].astype(F32), 0.0)
    step = WIDE // 4
    for t in range(TILES):
        lane = slice(t * LANES, (t + 1) * LANES)
        taps = weights[:, pl.ds(pl.multiple_of(x * BLOCK + t * LANES, LANES), LANES)]

        for row in range(0, WIDE, step):
            convolved[row : row + step, lane] = filter_rows(
                padded, lane, taps, row, step, {k: k for k in range(TAPS)}
            )

    count = jnp.clip(length - z * FRAMES, 0, FRAMES).astype(F32)
    keep = valid_rows(z * FRAMES, FRAMES, length)
    lines = []
    spreads = []
    for t in range(TILES):
        lane = slice(t * LANES, (t + 1) * LANES)
        values = convolved[HALF : HALF + FRAMES, lane]
        mean = jnp.sum(jnp.where(keep, values, 0.0), axis=0, keepdims=True) / jnp.maximum(count, 1.0)
        centred = jnp.where(keep, values - mean, 0.0)
        lines.append(mean)
        spreads.append(jnp.sum(centred * centred, axis=0, keepdims=True))
    ones = jnp.ones((1, LANES), F32)
    message = jnp.concatenate(lines + spreads + [ones * language.astype(F32), ones * count], axis=0)
    payload[...] = jnp.broadcast_to(message[None], (MEMBERS, 8, LANES))


def back_body(facts, first, second, third, fourth, own_half, other_half, back, weight):
    x, core = facts[0], facts[4]
    weight[at(core, SHARE), :] = own_half[...]
    weight[at(1 - core, SHARE), :] = other_half[...]
    for k, piece in enumerate((first, second, third, fourth)):
        j = lax.rem(x - k + PARTS, PARTS)
        result = dot(piece[...], weight[...], ((1,), (1,)))
        back[pl.ds(pl.multiple_of(HALF + j * OWN, HALF), OWN), :] = result[0:OWN]
        rim = pl.multiple_of(edge_row(j, 0, HALF + FRAMES, WIDE), HALF)
        back[pl.ds(rim, HALF), :] = result[OWN : OWN + HALF]


def combine(gathered, language):
    same = gathered[:, 6, :] == language.astype(F32)
    counts = jnp.where(same, gathered[:, 7, :], 0.0)
    total = jnp.maximum(jnp.sum(counts, axis=0, keepdims=True), 1.0)
    return same, counts, total


def chosen_row(table, index):
    here = lax.broadcasted_iota(jnp.int32, table.shape, 0) == index
    return jnp.sum(jnp.where(here, table, 0.0), axis=0, keepdims=True)


def act_body(facts, gathered, convolved, back, gains, biases, kept, sent, normed, grad, inverses, payload, active):
    x, z, length, language = facts[0], facts[1], facts[2], facts[3]
    same, counts, total = combine(gathered, language)
    spans = ((0, HALF), (HALF, FRAMES), (HALF + FRAMES, HALF))
    sums = [None] * 8
    sums[6] = sums[7] = jnp.zeros((1, LANES), F32)
    scales = []
    for t in range(TILES):
        lane = slice(t * LANES, (t + 1) * LANES)
        wide_lane = pl.ds(pl.multiple_of(x * BLOCK + t * LANES, LANES), LANES)
        means = gathered[:, t, :]
        average = jnp.sum(means * counts, axis=0, keepdims=True) / total
        spread = jnp.where(same, gathered[:, TILES + t, :], 0.0)
        away = means - average
        variance = jnp.sum(spread + counts * (away * away), axis=0, keepdims=True) / total
        inverse = lax.rsqrt(variance + EPSILON)
        scales.append(inverse)
        gain = chosen_row(gains[:, wide_lane], language)
        bias = chosen_row(biases[:, wide_lane], language)
        for part, (row, size) in enumerate(spans):
            step = min(size, 128)
            first = second = jnp.zeros((1, LANES), F32)
            for at_row in range(0, size, step):
                here = slice(row + at_row, row + at_row + step)
                keep = valid_rows(z * FRAMES - HALF + row + at_row, step, length)
                value = (convolved[here, lane] - average) * inverse
                pre = value * gain + bias
                gate = 1.0 / (1.0 + jnp.exp(-pre))
                upstream = back[here, lane]
                slope = jnp.where(keep, upstream * gate * (1.0 + pre * (1.0 - gate)), 0.0) * gain
                normed[here, lane] = value
                grad[here, lane] = slope
                if part == 1:
                    active[at_row : at_row + step, lane] = jnp.where(keep, pre * gate, 0.0).astype(BF16)
                    first = first + jnp.sum(slope, axis=0, keepdims=True)
                    second = second + jnp.sum(slope * value, axis=0, keepdims=True)
            if part == 1:
                sums[t], sums[TILES + t] = first, second
    payload[...] = jnp.broadcast_to(jnp.concatenate(sums, axis=0)[None], (MEMBERS, 8, LANES))
    first_core = facts[4] == 0
    kept[...] = jnp.where(first_core, active[:, :SHARE], active[:, SHARE:])
    sent[...] = jnp.where(first_core, active[:, SHARE:], active[:, :SHARE])
    inverses[...] = jnp.concatenate(scales + [sums[6]] * (8 - TILES), axis=0)


def grad_body(facts, gathered, sums, normed, grad, inverses, weights, first, second, third, fourth, rounded, result):
    x, z, length, language = facts[0], facts[1], facts[2], facts[3]
    same, counts, total = combine(gathered, language)
    keep = valid_rows(z * FRAMES - HALF, WIDE, length)
    step = FRAMES // 4
    for t in range(TILES):
        lane = slice(t * LANES, (t + 1) * LANES)
        shift = jnp.sum(jnp.where(same, sums[:, t, :], 0.0), axis=0, keepdims=True) / total
        scale = jnp.sum(jnp.where(same, sums[:, TILES + t, :], 0.0), axis=0, keepdims=True) / total
        inverse = inverses[t : t + 1, :]
        value = inverse * (grad[:, lane] - shift - normed[:, lane] * scale)
        rounded[:, lane] = jnp.where(keep, value, 0.0).astype(BF16).astype(F32)
    for t in range(TILES):
        lane = slice(t * LANES, (t + 1) * LANES)
        taps = weights[:, pl.ds(pl.multiple_of(x * BLOCK + t * LANES, LANES), LANES)]

        for row in range(0, FRAMES, step):
            value = filter_rows(rounded, lane, taps, row, step, {TAPS - k: k for k in range(TAPS)})
            inside = valid_rows(z * FRAMES + row, step, length)
            result[row : row + step, lane] = jnp.where(inside, value, 0.0)

    for k, piece in enumerate((first, second, third, fourth)):
        j = lax.rem(x + k, PARTS)
        piece[...] = result[at(j, OWN), :].astype(BF16)


def lanes_body(facts, first, second, third, fourth, joined):
    x = facts[0]
    for k, piece in enumerate((first, second, third, fourth)):
        j = lax.rem(x - k + PARTS, PARTS)
        joined[:, pl.ds(pl.multiple_of(j * BLOCK, LANES), BLOCK)] = piece[...]


def out_body(facts, mine, theirs, own_half, other_half, kept, first, second, third):
    x = facts[0]
    for k, piece in enumerate((kept, first, second, third)):
        rows = at(lax.rem(x + k, PARTS), OWN)
        total = dot(mine[rows, :], own_half[...], ((1,), (0,))) + dot(theirs[rows, :], other_half[...], ((1,), (0,)))
        piece[...] = total.astype(piece.dtype)


def product_body(facts, mine, theirs, first, second, third, fourth, kept, *sent):
    x = facts[0]
    for half in (theirs, mine):
        total = jnp.zeros((SHARE, CHANNELS), F32)
        for k, piece in enumerate((first, second, third, fourth)):
            j = lax.rem(x - k + PARTS, PARTS)
            total = total + dot(half[at(j, OWN), :], piece[0:OWN, :], ((0,), (0,)))
        if half is mine:
            kept[...] = total
        else:
            for n, target in enumerate(sent):
                target[...] = total[n * STRIP : (n + 1) * STRIP].astype(BF16)


def slots(q):
    row = lax.broadcasted_iota(jnp.int32, (SENT, 1), 0)
    inner = lax.rem(row, SLOT)
    wanted = jnp.where(inner // ROWS == q, row // SLOT * ROWS + lax.rem(inner, ROWS), -1)
    return (lax.broadcasted_iota(jnp.int32, (SENT, SHARE), 1) == wanted).astype(BF16)


def tile_at(q, g):
    start = (FOLD * g + q) * LANES
    return slice(start, start + LANES)


def folded(block, q):
    return jnp.concatenate([block[:, tile_at(q, g)] for g in range(TILES)], axis=1)


def copies_body(row_block, copies):
    inner = lax.rem(lax.broadcasted_iota(jnp.int32, (SENT, ROWS), 0), SLOT)
    column = lax.broadcasted_iota(jnp.int32, (SENT, ROWS), 1)
    total = jnp.zeros((SENT, BLOCK), F32)
    for q in range(FOLD):
        choose = (inner == q * ROWS + column).astype(BF16)
        total = total + dot(choose, folded(row_block[...], q), ((1,), (0,)))
    copies[...] = total.astype(BF16)


def weight_body(rows, half):
    for q in range(FOLD):
        part = dot(slots(q), rows[...], ((0,), (0,))).astype(BF16)
        for g in range(TILES):
            half[:, tile_at(q, g)] = part[:, g * LANES : (g + 1) * LANES]


def spread_body(kept, first, second, third, fourth, spread):
    other = jnp.concatenate([strip[...].astype(F32) for strip in (first, second, third, fourth)], axis=0)
    both = (kept[...] + other).astype(BF16)
    total = jnp.zeros((SENT, BLOCK), F32)
    for q in range(FOLD):
        total = total + dot(slots(q), folded(both, q), ((1,), (0,)))
    spread[...] = total.astype(BF16)


def unfold_body(sums, rows):
    for q in range(FOLD):
        for g in range(TILES):
            rows[:, tile_at(q, g)] = sums[q * ROWS : (q + 1) * ROWS, g * LANES : (g + 1) * LANES]


def around_x(piece, shift):
    size = AXES["x"]
    return lax.ppermute(piece, "x", [(i, (i + shift) % size) for i in range(size)])


def other_core(block):
    return lax.ppermute(block, "c", [(0, 1), (1, 0)])


def swap_xy(block):
    pairs = [(y * 4 + x, x * 4 + y) for y in range(4) for x in range(4)]
    return lax.ppermute(block, ("y", "x"), pairs)


def wait_for(value, *others):
    return lax.optimization_barrier((value,) + others)[0]


def between_blocks(rows):
    ends = [(4 * z + 3, 4 * z + 4) for z in range(AXES["z"] - 1)]
    return lax.ppermute(rows, ("z", "x"), ends + [(b, a) for a, b in ends])


def exchange(payload, axes):
    return lax.all_to_all(payload, axes, 0, 0, tiled=True)


def on_device(glu_out, conv_weight, bn_gain, bn_bias, w_out, cotangent, language, length):
    glu, cot = glu_out[0], cotangent[0]
    x, y, z, core = (lax.axis_index(axis) for axis in ("x", "y", "z", "c"))
    facts = jnp.stack([x, z, length[0], language[0], core, y]).astype(jnp.int32)

    last = x == PARTS - 1
    rim = jnp.concatenate(
        [
            lax.dynamic_slice_in_dim(glu, jnp.where(last, OWN - TAPS, 0), TAPS, 0),
            lax.dynamic_slice_in_dim(cot, jnp.where(last, OWN - HALF, 0), HALF, 0),
        ],
        axis=0,
    )
    rim = between_blocks(rim)
    swapped = swap_xy(w_out)

    pieces, slices = [], []
    for k in range(PARTS):
        column = lax.rem(x + k, PARTS) * BLOCK
        own = lax.dynamic_slice(glu, (0, column), (OWN, BLOCK))
        piece = jnp.concatenate([own, lax.dynamic_slice(rim, (0, column), (TAPS, BLOCK))], axis=0)
        slices.append(piece)
        pieces.append(around_x(piece, k) if k else piece)
    copies = small(copies_body, (SENT, BLOCK), BF16)(wait_for(swapped, *slices))
    rows = exchange(wait_for(copies, *pieces), ("z", "y"))
    cot = wait_for(jnp.concatenate([cot, rim[TAPS:]], axis=0), copies, *pieces)
    cots = [cot] + [around_x(cot, k) for k in range(1, PARTS)]
    convolved, payload = call(
        conv_body,
        [((WIDE, BLOCK), F32), ((MEMBERS, 8, LANES), F32)],
        [pltpu.VMEM((FRAMES + 3 * TAPS, BLOCK), F32)],
        cost=20,
    )(facts, wait_for(pieces[0], cots[1]), *pieces[1:], conv_weight)

    (half,) = call(weight_body, [((SHARE, CHANNELS), BF16)], scalars=0)(wait_for(rows, payload))
    gathered = exchange(wait_for(payload, *cots), STATS)
    other_half = other_core(half)
    (back,) = call(back_body, [((WIDE + HALF, BLOCK), F32)], [pltpu.VMEM((BLOCK, CHANNELS), BF16)], cost=3)(
        facts, *cots, half, other_half
    )

    kept, sent, normed, grad, inverses, payload = staged_call(
        act_body,
        [
            ((FRAMES, SHARE), BF16),
            ((FRAMES, SHARE), BF16),
            ((WIDE, BLOCK), F32),
            ((WIDE, BLOCK), F32),
            ((8, LANES), F32),
            ((MEMBERS, 8, LANES), F32),
        ],
        [pltpu.VMEM((FRAMES, BLOCK), BF16)],
        cost=2,
    )(facts, gathered, convolved, back, bn_gain, bn_bias)
    sums = exchange(payload, STATS)

    output, *others = call(out_body, [((OWN, CHANNELS), F32)] + [((OWN, CHANNELS), BF16)] * (PARTS - 1))(
        facts, kept, sent, half, other_half
    )
    arrived = [around_x(piece, k + 1) for k, piece in enumerate(others)]

    kept, *sent = call(product_body, [((SHARE, CHANNELS), F32)] + [((STRIP, CHANNELS), BF16)] * 4)(
        facts, wait_for(kept, *others), sent, *cots
    )
    (spread,) = call(spread_body, [((SENT, BLOCK), BF16)], scalars=0)(kept, *[other_core(strip) for strip in sent])
    spread = exchange(spread, ("z", "y")).reshape(32, SLOT, BLOCK)
    spread = swap_xy(jnp.sum(spread.astype(F32), axis=0))
    (weight_grad,) = call(unfold_body, [((ROWS, CHANNELS), F32)], scalars=0)(spread)

    pieces = call(
        grad_body,
        [((OWN, BLOCK), BF16)] * PARTS,
        [pltpu.VMEM((WIDE, BLOCK), F32), pltpu.VMEM((FRAMES, BLOCK), F32)],
        cost=5,
    )(facts, gathered, wait_for(sums, *arrived), normed, grad, inverses, conv_weight)
    for piece in arrived:
        output = output + wait_for(piece, *pieces).astype(F32)
    output = output.astype(BF16)
    pieces = [pieces[0]] + [around_x(pieces[k], k) for k in range(1, PARTS)]
    (input_grad,) = call(lanes_body, [((OWN, CHANNELS), BF16)])(facts, *pieces)
    return output[None], weight_grad, input_grad[None]


def solution(mesh):
    fine = Mesh(mesh.devices.reshape(tuple(AXES.values())), tuple(AXES))
    dp, seq = ("y", "c"), ("z", "x")
    placed = (
        P(dp, seq, None),
        P(),
        P(),
        P(),
        P(dp + seq, None),
        P(dp, seq, None),
        P(dp),
        P(dp),
    )
    return jax.shard_map(
        on_device,
        mesh=fine,
        in_specs=placed,
        out_specs=(P(dp, seq, None), P(dp + seq, None), P(dp, seq, None)),
        check_vma=False,
    )
```
